128 devices in a mesh: node: 8 (over x, core), blk: 16 (over z, y).
Axes of the slice: x: 4, y: 4, z: 4, core: 2. Of those that a mesh axis runs over, the one named last changes fastest.
Arguments:
- tokens: bfloat16 [1792, 7168], P(('node', 'blk')), may hold values from -6 to 6
- out_grad: bfloat16 [1792, 7168], P(('node', 'blk')), may hold values from -6 to 6
- expert_ids: int32 [1792, 4], P(('node', 'blk')), may hold values from 0 to 7, all different within a row; in each aligned block of 14 rows (0 to 13, 14 to 27, ...) at most 7 rows name the same one
- gates: bfloat16 [1792, 4], P(('node', 'blk')), may hold values from 0.099609375 to 1
- w_gate: bfloat16 [8, 7168, 2048], P('node', None, 'blk'), may hold values from -0.0625 to 0.0625
- w_up: bfloat16 [8, 7168, 2048], P('node', None, 'blk'), may hold values from -0.0625 to 0.0625
- w_down: bfloat16 [8, 2048, 7168], P('node', 'blk'), may hold values from -0.125 to 0.125
Outputs:
- input_grad: bfloat16 [1792, 7168], P(('node', 'blk'))
- gate_grad: bfloat16 [8, 7168, 2048], P('node', None, 'blk')
- up_grad: bfloat16 [8, 7168, 2048], P('node', None, 'blk')
- down_grad: bfloat16 [8, 2048, 7168], P('node', 'blk')
The draws below stay inside these ranges and needn't reach their ends.
Inputs may be any that keep to these rules, and one draw needn't show every extreme that they name: `expert_ids`: each token names 4 different experts. Among the 14 tokens of one device at most 7 name any one expert, and in some device exactly 7 name one expert.
All inputs are finite; a program needn't handle non-finite values.
Results may differ from the reference program's by a relative error of at most 0.02.
Values may be sent and summed in bfloat16 or wider, within the bound.
No kernel may reach another device: no remote copies, remote signals or barrier semaphores. Data moves between devices by JAX's collectives and lax.ppermute only.
A program may use at most 192 MiB of HBM per device.

```python
import math
import jax
import jax.numpy as jnp
import numpy as np
from jax import lax

D = 7168
FF = 2048
TOK_DEV = 14
TOPK = 4
CAP = 7
EXPERTS = 8
TOKENS = 1792
N_NODE = 8
N_BLK = 16


def levels(rng, shape, cuts, low, high):
    def one(dim, blocks):
        draws = jax.random.uniform(jax.random.fold_in(jax.random.fold_in(rng, 6), dim), (blocks,), jnp.float32, low / len(cuts), high / len(cuts))
        return jnp.repeat(jnp.exp(draws), shape[dim] // blocks).reshape((-1,) + (1,) * (len(shape) - dim - 1))

    factor_of = one(*cuts[0])
    for cut in cuts[1:]:
        factor_of = factor_of * one(*cut)
    return factor_of


def deal_out(rng, own, number, rows, count, top, bound, slope):
    order = jax.random.permutation(rng, count)
    crowded, ordinary = load_shares(count, rows * top, bound, slope, True), load_shares(count, rows * top, bound, slope, False)
    places = jnp.arange(count)

    def named(lengths, rotation):
        used = int((lengths > 0).sum())
        fixed = max(1, used // 4)
        shifted = fixed + (places - fixed + rotation * (used - fixed)) % max(1, count - fixed)
        return jnp.zeros((count,), jnp.int32).at[order[jnp.where(places < fixed, places, shifted)]].set(jnp.asarray(lengths, jnp.int32))

    lengths = jnp.where(number % 4 == 0, named(crowded, number // 4), named(ordinary, number - number // 4 - 1))
    mixed = jax.random.permutation(jax.random.fold_in(own, 3), count)
    donor, receiver = mixed[0:count // 2 * 2:2], mixed[1:count // 2 * 2:2]
    room = jnp.minimum(lengths[donor] - 1, bound - lengths[receiver]) // 2
    room = jnp.where((donor == order[0]) | (receiver == order[0]) | (lengths[receiver] == 0), 0, jnp.maximum(room, 0))
    shifted = jax.random.randint(jax.random.fold_in(own, 4), (count // 2,), 0, 1 << 20) % (room + 1)
    lengths = lengths.at[donor].add(-shifted).at[receiver].add(shifted)
    labels = jnp.searchsorted(jnp.cumsum(lengths), jnp.arange(rows * top), side="right").astype(jnp.int32)
    grid = labels.reshape(top, rows).T
    grid = grid[jax.random.permutation(jax.random.fold_in(own, 1), rows)]
    rotation = jax.random.randint(jax.random.fold_in(own, 2), (rows, 1), 0, top)
    return jnp.take_along_axis(grid, (jnp.arange(top)[None, :] + rotation) % top, axis=1)


def load_shares(count, total, most, slope, full):
    weights = [(1 << 20) // math.isqrt(grade ** slope) + 1 for grade in range(1, count + 1)]
    largest = most if full else min(most, max(-(-total // count), total * weights[0] // sum(weights)))
    least = 1 if total - largest >= count - 1 else 0
    holding, surplus = [largest] + [least] * (count - 1), total - largest - least * (count - 1)
    while surplus > 0:
        free = [i for i in range(1, count) if holding[i] < largest] or [i for i in range(1, count) if holding[i] < most]
        whole, remaining = sum([weights[i] for i in free]), surplus
        for i in free:
            more = min(most - holding[i], max(1, remaining * weights[i] // whole), surplus)
            holding[i] = holding[i] + more
            surplus = surplus - more
    return np.array(holding)


def bell_draw(rng, dims, width, reach, cuts=(), kind=jnp.bfloat16):
    result = width * jax.random.normal(rng, dims, jnp.float32)
    if cuts:
        result = result * levels(rng, dims, cuts, -0.22, 0.18)
    return jnp.clip(result, -reach, reach).astype(kind)


def setup_inputs(seed: int = 0) -> dict:
    streams_of = jax.random.split(jax.random.key(seed), 8)
    tokens = bell_draw(streams_of[0], (TOKENS, D), 1.0, 6.0, ((0, 128),))
    out_grad = bell_draw(streams_of[1], (TOKENS, D), 1.0, 6.0, ((0, 128),))
    expert_ids_keys = jax.random.split(jax.random.fold_in(streams_of[2], 1), TOKENS // TOK_DEV)
    expert_ids_turns = jax.random.permutation(jax.random.fold_in(streams_of[2], 3), TOKENS // TOK_DEV)
    expert_ids = jax.vmap(lambda own, number: deal_out(jax.random.fold_in(streams_of[2], 2), own, number, TOK_DEV, EXPERTS, TOPK, CAP, 2))(expert_ids_keys, expert_ids_turns).reshape((TOKENS, TOPK))
    gates = jnp.clip(0.099609375 + 0.9003906 * jax.random.uniform(streams_of[3], (TOKENS, TOPK), jnp.float32) ** levels(streams_of[3], (TOKENS, TOPK), ((0, 128),), -0.2, 0.2), 0.099609375, 1.0).astype(jnp.bfloat16)
    w_gate = bell_draw(streams_of[4], (EXPERTS, D, FF), D ** -0.5, 0.0625, ((0, 8), (2, 16)))
    w_up = bell_draw(streams_of[5], (EXPERTS, D, FF), D ** -0.5, 0.0625, ((0, 8), (2, 16)))
    w_down = bell_draw(streams_of[6], (EXPERTS, FF, D), FF ** -0.5, 0.125, ((0, 8), (1, 16)))
    return dict(tokens=tokens, out_grad=out_grad, expert_ids=expert_ids, gates=gates, w_gate=w_gate, w_up=w_up, w_down=w_down)


def expert_block(inputs):
    rows_x, rows_grad, gate_weight, up_weight, down_weight = inputs
    model_width = rows_x.shape[1]
    total_rows = rows_x.shape[0]
    pre_gate = jnp.dot(rows_x, gate_weight, preferred_element_type=jnp.float32)
    pre_up = jnp.dot(rows_x, up_weight, preferred_element_type=jnp.float32)
    act_grad = jnp.dot(rows_grad, down_weight.T, preferred_element_type=jnp.float32)
    sigmoid_gate = jax.nn.sigmoid(pre_gate)
    silu_gate = pre_gate * sigmoid_gate
    activation = (silu_gate * pre_up).astype(jnp.bfloat16)
    gate_delta = (act_grad * pre_up * sigmoid_gate * (1.0 + pre_gate * (1.0 - sigmoid_gate))).astype(jnp.bfloat16)
    up_delta = (act_grad * silu_gate).astype(jnp.bfloat16)
    block_width = FF // N_BLK
    gate_blocks = gate_delta.astype(jnp.float32).reshape(total_rows, N_BLK, block_width)
    up_blocks = up_delta.astype(jnp.float32).reshape(total_rows, N_BLK, block_width)
    gate_table = gate_weight.astype(jnp.float32).reshape(model_width, N_BLK, block_width)
    up_table = up_weight.astype(jnp.float32).reshape(model_width, N_BLK, block_width)
    pieces = jnp.einsum('rbf,dbf->brd', gate_blocks, gate_table) + jnp.einsum('rbf,dbf->brd', up_blocks, up_table)
    pieces = lax.optimization_barrier(pieces.astype(jnp.bfloat16))
    row_grad = jnp.sum(pieces.astype(jnp.float32), axis=0).astype(jnp.bfloat16)
    gate_grad = jnp.dot(rows_x.T, gate_delta, preferred_element_type=jnp.float32).astype(jnp.bfloat16)
    up_grad = jnp.dot(rows_x.T, up_delta, preferred_element_type=jnp.float32).astype(jnp.bfloat16)
    down_grad = jnp.dot(activation.T, rows_grad, preferred_element_type=jnp.float32).astype(jnp.bfloat16)
    return row_grad, gate_grad, up_grad, down_grad


def reference(tokens, out_grad, expert_ids, gates, w_gate, w_up, w_down):
    groups = N_NODE * N_BLK
    expert_count = N_NODE
    model_width = tokens.shape[1]
    token_blocks = tokens.reshape(groups, TOK_DEV, model_width).astype(jnp.float32)
    grad_blocks = out_grad.reshape(groups, TOK_DEV, model_width).astype(jnp.float32)
    onehot = expert_ids.reshape(groups, TOK_DEV, TOPK)[..., None] == jnp.arange(expert_count, dtype=jnp.int32)
    chosen = jnp.sum(onehot.astype(jnp.int32), axis=2)
    gate_sum = jnp.sum(onehot.astype(jnp.float32) * gates.reshape(groups, TOK_DEV, TOPK).astype(jnp.float32)[..., None], axis=2)
    slot_rank = jnp.cumsum(chosen, axis=1) - chosen
    slot_mask = ((chosen[..., None] == 1) & (slot_rank[..., None] == jnp.arange(CAP, dtype=jnp.int32))).astype(jnp.float32)
    packed_x = jnp.einsum('gtec,gtd->egcd', slot_mask, token_blocks).astype(jnp.bfloat16)
    packed_grad = jnp.einsum('gtec,gtd->egcd', slot_mask, grad_blocks)
    packed_gate = jnp.einsum('gtec,gte->egc', slot_mask, gate_sum)
    scaled = (packed_gate[..., None] * packed_grad).astype(jnp.bfloat16)
    inputs = (packed_x.reshape(expert_count, groups * CAP, model_width), scaled.reshape(expert_count, groups * CAP, model_width), w_gate, w_up, w_down)
    row_grad, gate_grad, up_grad, down_grad = lax.map(expert_block, inputs)
    row_grad = row_grad.reshape(expert_count, groups, CAP, model_width).astype(jnp.float32)
    input_grad = jnp.einsum('gtec,egcd->gtd', slot_mask, row_grad).astype(jnp.bfloat16)
    return input_grad.reshape(groups * TOK_DEV, model_width), gate_grad, up_grad, down_grad
```

```python
import jax
import jax.numpy as jnp
import numpy as np
from jax import lax
from jax.sharding import PartitionSpec as P

ALL = ("node", "blk")
SIZES = (4, 2, 4, 4)
AXIS = {"x": 0, "z": 2, "y": 3}
ORDERS = (("x", "y", "z"), ("y", "z", "x"), ("z", "x", "y"))
PARTS = ((0, 9), (9, 18), (18, 28))
TOK = 14
UNIT = 24


def shifted(axis, by_core):
    pairs = []
    for at in np.ndindex(*SIZES):
        to = list(at)
        to[axis] = (to[axis] + by_core[at[1]]) % 4
        pairs.append((int(np.ravel_multi_index(at, SIZES)), int(np.ravel_multi_index(to, SIZES))))
    return pairs


def swap_pairs():
    pairs = []
    for at in np.ndindex(*SIZES):
        to = (at[0], 1 - at[1], at[2], at[3])
        pairs.append((int(np.ravel_multi_index(at, SIZES)), int(np.ravel_multi_index(to, SIZES))))
    return pairs


def swap(value):
    return lax.ppermute(value, ALL, swap_pairs())


def hop(value, axis, steps=1):
    return lax.ppermute(value, ALL, shifted(AXIS[axis], (steps, -steps)))


def gather_ring(value, axis):
    held = [value]
    for _ in range(3):
        held.append(hop(held[-1], axis))
    return held


def reduce_ring(terms, axis):
    total = terms[3]
    for k in (2, 1, 0):
        arrived = hop(total, axis, -1)
        total = (arrived.astype(jnp.float32) + terms[k].astype(jnp.float32)).astype(jnp.bfloat16)
    return total


def offset(k, core):
    return (-k) % 4 if core == 0 else k


def place(core, pick):
    tables = []
    for c in (0, 1):
        rows, width = pick(c)
        table = np.zeros((len(rows), width), np.float32)
        for r, column in enumerate(rows):
            if column >= 0:
                table[r, column] = 1
        tables.append(table)
    return jnp.where(core == 0, jnp.asarray(tables[0], jnp.bfloat16), jnp.asarray(tables[1], jnp.bfloat16))


def move(table, value):
    return jnp.dot(table, value, preferred_element_type=jnp.float32).astype(jnp.bfloat16)


def pick_first(c):
    rows = []
    for lo, hi in PARTS:
        part = []
        for kind in (0, 1):
            for i in range(lo, hi):
                source = 0 if i // TOK == c else 2 * TOK
                part.append(source + kind * TOK + i % TOK)
        rows += part + [-1] * (UNIT - len(part))
    return rows, 4 * TOK


def pick_second(n):
    def pick(c):
        rows = []
        for kind in (0, 1):
            for o in range(4):
                k = [k for k in range(4) if offset(k, c) == o][0]
                rows += [k * UNIT + kind * n + i for i in range(n)]
        return rows, 4 * UNIT

    return pick


def pick_third(n):
    def pick(c):
        rows = []
        for kind in (0, 1):
            for o in range(4):
                k = [k for k in range(4) if offset(k, c) == o][0]
                rows += [k * 8 * n + kind * 4 * n + i for i in range(4 * n)]
        return rows, 32 * n

    return pick


def pick_split(n, held, padded):
    def pick(c):
        rows = []
        for k in range(4):
            o = offset(k, c)
            rows += [o * n + i for i in range(n)] + [-1] * (padded - n)
        return rows, held

    return pick


def pick_last(c):
    rows = []
    for core in (c, 1 - c):
        for t in range(TOK):
            i = core * TOK + t
            p = [p for p in range(3) if PARTS[p][0] <= i < PARTS[p][1]][0]
            rows.append(16 * p + i - PARTS[p][0])
        rows += [-1, -1]
    return rows, 48


def row_tokens(at, core):
    place_of = {"x": at[0], "z": at[1], "y": at[2]}
    result = []
    for k in range(4):
        for p, (lo, hi) in enumerate(PARTS):
            n = hi - lo
            grids = np.meshgrid(np.arange(4), np.arange(4), np.arange(lo, hi), indexing="ij")
            second, first, row = (g.reshape(-1) for g in grids)
            spot = dict(place_of)
            spot[ORDERS[p][0]] = (place_of[ORDERS[p][0]] + first) % 4
            spot[ORDERS[p][1]] = (place_of[ORDERS[p][1]] + second) % 4
            third = jnp.where(core == 0, (-k) % 4, k)
            spot[ORDERS[p][2]] = (place_of[ORDERS[p][2]] + third) % 4
            device = ((spot["x"] * 2 + row // TOK) * 4 + spot["z"]) * 4 + spot["y"]
            result.append(device * TOK + row % TOK)
    return jnp.concatenate([jnp.broadcast_to(r, (r.shape[0],)) for r in result])


def halves(value, core, axis):
    size = value.shape[axis] // 2
    low = lax.slice_in_dim(value, 0, size, axis=axis)
    high = lax.slice_in_dim(value, size, 2 * size, axis=axis)
    return jnp.where(core == 0, low, high), jnp.where(core == 0, high, low)


def joined(own, other, core, axis):
    return jnp.where(core == 0, jnp.concatenate([own, other], axis), jnp.concatenate([other, own], axis))


def on_device(tokens, out_grad, expert_ids, gates, w_gate, w_up, w_down):
    node, blk = lax.axis_index("node"), lax.axis_index("blk")
    x, core, z, y = node // 2, node % 2, blk // 4, blk % 4

    own, other = halves(jnp.concatenate([tokens, out_grad], 0), core, 1)
    rows = jnp.concatenate([own, swap(other)], 0)
    units = move(place(core, pick_first), rows)

    w_own, w_other = halves(jnp.concatenate([w_gate[0], w_up[0]], 1), core, 0)
    w_in = jnp.concatenate([w_own, swap(w_other)], 1)
    d_own, d_other = halves(w_down[0], core, 1)
    w_out = jnp.concatenate([d_own, swap(d_other)], 0)

    onehot = expert_ids[:, :, None] == jnp.arange(8, dtype=jnp.int32)
    gate_sum = jnp.sum(onehot.astype(jnp.float32) * gates.astype(jnp.float32)[:, :, None], axis=1)
    every = lax.all_gather(gate_sum.astype(jnp.bfloat16), ALL, axis=0, tiled=True)
    index = row_tokens((x, z, y), core)
    chosen = (jnp.arange(8) == node).astype(jnp.bfloat16), (jnp.arange(8) == node + 1 - 2 * core).astype(jnp.bfloat16)
    pair = jnp.dot(every, jnp.stack(chosen, 1), preferred_element_type=jnp.float32).astype(jnp.bfloat16)
    spread = (index[:, None] == jnp.arange(every.shape[0], dtype=jnp.int32)[None, :]).astype(jnp.bfloat16)
    row_gate = jnp.dot(spread, pair, preferred_element_type=jnp.float32).reshape(4, 448, 2)

    rows_x, rows_g = [], []
    for p, (lo, hi) in enumerate(PARTS):
        n = hi - lo
        held = gather_ring(units[p * UNIT : (p + 1) * UNIT], ORDERS[p][0])
        unit = move(place(core, pick_second(n)), jnp.concatenate(held, 0))
        held = gather_ring(unit, ORDERS[p][1])
        unit = move(place(core, pick_third(n)), jnp.concatenate(held, 0))
        rows_x.append(gather_ring(unit[: 16 * n], ORDERS[p][2]))
        rows_g.append(gather_ring(unit[16 * n :], ORDERS[p][2]))

    pre, act, arrived = [], [], []
    for k in range(4):
        pre.append(jnp.concatenate([jnp.dot(r[k], w_in, preferred_element_type=jnp.float32) for r in rows_x], 0))
        act.append(
            jnp.concatenate(
                [
                    lax.dot_general(r[k], w_out, (((1,), (1,)), ((), ())), preferred_element_type=jnp.float32)
                    for r in rows_g
                ],
                0,
            )
        )
        arrived.append(swap(jnp.concatenate([pre[k][:, 256:], pre[k][:, :256], act[k][:, 128:], act[k][:, :128]], 1)))

    deltas, activations, pieces = [None] * 4, [None] * 4, [None] * 4
    for k in (3, 2, 1, 0):
        both = jnp.concatenate([pre[k], act[k]], 1) + arrived[(4 - k) % 4]
        delta, activation = [], []
        for e in (0, 1):
            gate = row_gate[k, :, e : e + 1]
            pre_gate = both[:, 256 * e : 256 * e + 128]
            pre_up = both[:, 256 * e + 128 : 256 * e + 256]
            act_grad = gate * both[:, 512 + 128 * e : 640 + 128 * e]
            sigmoid_gate = jax.nn.sigmoid(pre_gate)
            silu_gate = pre_gate * sigmoid_gate
            activation.append((gate * (silu_gate * pre_up)).astype(jnp.bfloat16))
            delta.append(
                (act_grad * pre_up * sigmoid_gate * (1.0 + pre_gate * (1.0 - sigmoid_gate))).astype(jnp.bfloat16)
            )
            delta.append((act_grad * silu_gate).astype(jnp.bfloat16))
        deltas[k] = jnp.concatenate(delta, 1)
        activations[k] = jnp.concatenate(activation, 1)
        pieces[k] = lax.dot_general(
            deltas[k], w_in, (((1,), (1,)), ((), ())), preferred_element_type=jnp.float32
        ).astype(jnp.bfloat16)

    finished = []
    for p, (lo, hi) in enumerate(PARTS):
        n = hi - lo
        total = reduce_ring([pieces[k][16 * lo : 16 * hi] for k in range(4)], ORDERS[p][2])
        split = move(place(core, pick_split(4 * n, 16 * n, 40)), total)
        total = reduce_ring([split[40 * k : 40 * k + 40] for k in range(4)], ORDERS[p][1])
        split = move(place(core, pick_split(n, 40, 16)), total)
        finished.append(reduce_ring([split[16 * k : 16 * k + 16] for k in range(4)], ORDERS[p][0]))
    finished = move(place(core, pick_last), jnp.concatenate(finished, 0))
    input_grad = joined(finished[:TOK], swap(finished[16 : 16 + TOK]), core, 1)

    all_x = jnp.concatenate([r[k] for k in range(4) for r in rows_x], 0)
    all_g = jnp.concatenate([r[k] for k in range(4) for r in rows_g], 0)
    w_grad = lax.dot_general(
        all_x, jnp.concatenate(deltas, 0), (((0,), (0,)), ((), ())), preferred_element_type=jnp.float32
    ).astype(jnp.bfloat16)
    d_grad = lax.dot_general(
        jnp.concatenate(activations, 0), all_g, (((0,), (0,)), ((), ())), preferred_element_type=jnp.float32
    ).astype(jnp.bfloat16)
    w_grad = joined(w_grad[:, :256], swap(w_grad[:, 256:]), core, 0)
    down_grad = joined(d_grad[:128], swap(d_grad[128:]), core, 1)
    return input_grad, w_grad[:, :128][None], w_grad[:, 128:][None], down_grad[None]


def solution(mesh):
    rows, deep, wide = P(ALL, None), P("node", None, "blk"), P("node", "blk", None)
    return jax.shard_map(
        on_device,
        mesh=mesh,
        in_specs=(rows, rows, rows, rows, deep, deep, wide),
        out_specs=(rows, deep, deep, wide),
        check_vma=False,
    )
```

```python
import jax
import jax.numpy as jnp
import numpy as np
from jax import lax
from jax.sharding import PartitionSpec as P

ALL = ("node", "blk")
SIZES = (4, 2, 4, 4)
AXIS = {"x": 0, "z": 2, "y": 3}
ORDERS = (("x", "y", "z"), ("y", "z", "x"), ("z", "x", "y"))
PARTS = ((0, 9), (9, 18), (18, 28))
TOK = 14
HALF = 3584
WIDE = HALF + 128
UNIT = 24
WINDOW = 5
FIRST, SECOND = (1, 3), (3, 1)
OWNERS = ((0, 1, 3, 2), (0, 3, 1, 2))


class Held:
    def __init__(self, value):
        self.value = value


class Link:
    def __init__(self):
        self.sent = []

    def send(self, value, pairs):
        if len(self.sent) >= WINDOW:
            before = self.sent[-WINDOW]
            value, before.value = lax.optimization_barrier((value, before.value))
        self.sent.append(Held(lax.ppermute(value, ALL, pairs)))
        return self.sent[-1]

    def swap(self, value):
        return self.send(value, PAIRS["core"])

    def hop(self, value, axis, turn):
        return self.send(value, PAIRS[axis, turn])

    def gather(self, values, axes):
        first = [self.hop(v, axis, 0) for v, axis in zip(values, axes)]
        second = [self.hop(v, axis, 1) for v, axis in zip(values, axes)]
        far = [self.hop(f.value, axis, 1) for f, axis in zip(first, axes)]
        return [[Held(v), f, s, d] for v, f, s, d in zip(values, first, second, far)]

    def reduce(self, terms, axes):
        second = [self.hop(t[2], axis, 1) for t, axis in zip(terms, axes)]
        far = [self.hop(t[3], axis, 1) for t, axis in zip(terms, axes)]
        first = [self.hop(added(t[1], f.value), axis, 0) for t, f, axis in zip(terms, far, axes)]
        return [added(t[0], s.value, f.value) for t, s, f in zip(terms, second, first)]


def added(*terms):
    total = terms[0].astype(jnp.float32)
    for term in terms[1:]:
        total = total + term.astype(jnp.float32)
    return total.astype(jnp.bfloat16)


def paired(target):
    pairs = []
    for at in np.ndindex(*SIZES):
        pairs.append((int(np.ravel_multi_index(at, SIZES)), int(np.ravel_multi_index(target(at), SIZES))))
    return pairs


def neighbour(axis, by_core):
    def target(at):
        to = list(at)
        to[axis] = to[axis] ^ by_core[at[1]]
        return tuple(to)

    return target


PAIRS = {"core": paired(lambda at: (at[0], 1 - at[1], at[2], at[3]))}
for _name, _axis in AXIS.items():
    PAIRS[_name, 0] = paired(neighbour(_axis, FIRST))
    PAIRS[_name, 1] = paired(neighbour(_axis, SECOND))


def place(core, pick):
    tables = []
    for c in (0, 1):
        rows, width = pick(c)
        table = np.zeros((len(rows), width), np.float32)
        for r, column in enumerate(rows):
            if column >= 0:
                table[r, column] = 1
        tables.append(table)
    return jnp.where(core == 0, jnp.asarray(tables[0], jnp.bfloat16), jnp.asarray(tables[1], jnp.bfloat16))


def move(table, value):
    return jnp.dot(table, value, preferred_element_type=jnp.float32).astype(jnp.bfloat16)


def pick_first(c):
    rows = []
    for lo, hi in PARTS:
        part = []
        for kind in (0, 1):
            for i in range(lo, hi):
                source = 0 if i // TOK == c else 2 * TOK
                part.append(source + kind * TOK + i % TOK)
        rows += part + [-1] * (UNIT - len(part))
    return rows, 4 * TOK


def pick_joined(n, stride):
    def pick(c):
        rows = []
        for kind in (0, 1):
            for j in range(4):
                rows += [OWNERS[c].index(j) * stride + kind * n + i for i in range(n)]
        return rows, 4 * stride

    return pick


def pick_split(n, held, padded):
    def pick(c):
        rows = []
        for q in range(4):
            rows += [OWNERS[c][q] * n + i for i in range(n)] + [-1] * (padded - n)
        return rows, held

    return pick


def pick_last(c):
    rows = []
    for core in (c, 1 - c):
        for t in range(TOK):
            i = core * TOK + t
            p = [p for p in range(3) if PARTS[p][0] <= i < PARTS[p][1]][0]
            rows.append(16 * p + i - PARTS[p][0])
        rows += [-1, -1]
    return rows, 48


def halves(value, core, axis):
    size = value.shape[axis] // 2
    low = lax.slice_in_dim(value, 0, size, axis=axis)
    high = lax.slice_in_dim(value, size, 2 * size, axis=axis)
    return jnp.where(core == 0, low, high), jnp.where(core == 0, high, low)


def joined(own, other, core, axis):
    return jnp.where(core == 0, jnp.concatenate([own, other], axis), jnp.concatenate([other, own], axis))


def on_device(tokens, out_grad, expert_ids, gates, w_gate, w_up, w_down):
    node = lax.axis_index("node")
    core = node % 2
    link = Link()
    sizes = [hi - lo for lo, hi in PARTS]

    onehot = expert_ids[:, :, None] == jnp.arange(8, dtype=jnp.int32)
    gate_sum = jnp.sum(onehot.astype(jnp.float32) * gates.astype(jnp.float32)[:, :, None], axis=1).astype(jnp.bfloat16)
    gate_sum = jnp.pad(jnp.concatenate([jnp.zeros_like(gate_sum), gate_sum], 0), ((0, 0), (0, 120)))
    own, other = halves(jnp.concatenate([tokens, out_grad], 0), core, 1)
    other = link.swap(jnp.concatenate([other, gate_sum], 1))
    rows = jnp.concatenate([jnp.concatenate([own, gate_sum], 1), other.value], 0)
    units = move(place(core, pick_first), rows)

    held = link.gather([units[p * UNIT : (p + 1) * UNIT] for p in range(3)], [o[0] for o in ORDERS])
    units = [
        move(place(core, pick_joined(n, UNIT)), jnp.concatenate([b.value for b in h], 0)) for n, h in zip(sizes, held)
    ]
    w_own, w_other = halves(jnp.concatenate([w_gate[0], w_up[0]], 1), core, 0)
    d_own, d_other = halves(w_down[0], core, 1)
    w_other = link.swap(w_other)
    d_other = link.swap(d_other)
    held = link.gather(units, [o[1] for o in ORDERS])
    units = [
        move(place(core, pick_joined(4 * n, 8 * n)), jnp.concatenate([b.value for b in h], 0))
        for n, h in zip(sizes, held)
    ]
    w_in = jnp.concatenate([w_own, w_other.value], 1)
    w_out = jnp.concatenate([d_own, d_other.value], 0)

    axes = [o[2] for o in ORDERS]
    blocks = [[Held(u) for u in units], None, None, None]
    chosen = (jnp.arange(128) == node).astype(jnp.bfloat16), (jnp.arange(128) == node + 1 - 2 * core).astype(jnp.bfloat16)
    chosen = jnp.stack(chosen, 1)

    def forward(q):
        x_rows = [b.value[: 16 * n, :HALF] for b, n in zip(blocks[q], sizes)]
        g_rows = [b.value[16 * n :, :HALF] for b, n in zip(blocks[q], sizes)]
        pre = [jnp.dot(r, w_in, preferred_element_type=jnp.float32) for r in x_rows]
        act = [
            lax.dot_general(r, w_out, (((1,), (1,)), ((), ())), preferred_element_type=jnp.float32) for r in g_rows
        ]
        return jnp.concatenate(pre, 0), jnp.concatenate(act, 0)

    def crossed(pre, act):
        return jnp.concatenate([pre[:, 256:], pre[:, :256], act[:, 128:], act[:, :128]], 1)

    def backward(q, sums, arrived):
        both = jnp.concatenate(sums, 1) + arrived
        row_gate = [b.value[16 * n :, HALF:] for b, n in zip(blocks[q], sizes)]
        row_gate = jnp.dot(jnp.concatenate(row_gate, 0), chosen, preferred_element_type=jnp.float32)
        delta, activation = [], []
        for e in (0, 1):
            gate = row_gate[:, e : e + 1]
            pre_gate = both[:, 256 * e : 256 * e + 128]
            pre_up = both[:, 256 * e + 128 : 256 * e + 256]
            act_grad = gate * both[:, 512 + 128 * e : 640 + 128 * e]
            sigmoid_gate = jax.nn.sigmoid(pre_gate)
            silu_gate = pre_gate * sigmoid_gate
            activation.append((gate * (silu_gate * pre_up)).astype(jnp.bfloat16))
            delta.append(
                (act_grad * pre_up * sigmoid_gate * (1.0 + pre_gate * (1.0 - sigmoid_gate))).astype(jnp.bfloat16)
            )
            delta.append((act_grad * silu_gate).astype(jnp.bfloat16))
        delta = jnp.concatenate(delta, 1)
        pieces = lax.dot_general(delta, w_in, (((1,), (1,)), ((), ())), preferred_element_type=jnp.float32)
        pieces = pieces.astype(jnp.bfloat16)
        return delta, jnp.concatenate(activation, 1), [pieces[16 * lo : 16 * hi] for lo, hi in PARTS]

    blocks[1] = [link.hop(b.value, axis, 0) for b, axis in zip(blocks[0], axes)]
    blocks[2] = [link.hop(b.value, axis, 1) for b, axis in zip(blocks[0], axes)]
    sums = [forward(0), None, None, None]
    arrived = [link.swap(crossed(*sums[0])), None, None, None]
    blocks[3] = [link.hop(b.value, axis, 1) for b, axis in zip(blocks[1], axes)]
    sums[1], sums[2] = forward(1), forward(2)
    both = link.swap(jnp.concatenate([crossed(*sums[2]), crossed(*sums[1])], 0))
    done = [backward(0, sums[0], arrived[0].value), None, None, None]
    done[2] = backward(2, sums[2], both.value[448:])
    second = [link.hop(t, axis, 1) for t, axis in zip(done[2][2], axes)]
    sums[3] = forward(3)
    arrived[3] = link.swap(crossed(*sums[3]))
    done[1] = backward(1, sums[1], both.value[:448])
    done[3] = backward(3, sums[3], arrived[3].value)
    far = [link.hop(t, axis, 1) for t, axis in zip(done[3][2], axes)]
    first = [link.hop(added(t, f.value), axis, 0) for t, f, axis in zip(done[1][2], far, axes)]
    totals = [added(t, s.value, f.value) for t, s, f in zip(done[0][2], second, first)]

    terms = [move(place(core, pick_split(4 * n, 16 * n, 40)), t) for n, t in zip(sizes, totals)]
    totals = link.reduce([[t[40 * q : 40 * q + 40] for q in range(4)] for t in terms], [o[1] for o in ORDERS])
    terms = [move(place(core, pick_split(n, 40, 16)), t) for n, t in zip(sizes, totals)]
    totals = link.reduce([[t[16 * q : 16 * q + 16] for q in range(4)] for t in terms], [o[0] for o in ORDERS])
    finished = move(place(core, pick_last), jnp.concatenate(totals, 0))
    arrived = link.swap(finished[16 : 16 + TOK])
    input_grad = joined(finished[:TOK], arrived.value, core, 1)

    all_x = jnp.concatenate([b.value[: 16 * n, :HALF] for q in range(4) for b, n in zip(blocks[q], sizes)], 0)
    all_g = jnp.concatenate([b.value[16 * n :, :HALF] for q in range(4) for b, n in zip(blocks[q], sizes)], 0)
    w_grad = lax.dot_general(
        all_x, jnp.concatenate([d[0] for d in done], 0), (((0,), (0,)), ((), ())), preferred_element_type=jnp.float32
    ).astype(jnp.bfloat16)
    d_grad = lax.dot_general(
        jnp.concatenate([d[1] for d in done], 0), all_g, (((0,), (0,)), ((), ())), preferred_element_type=jnp.float32
    ).astype(jnp.bfloat16)
    w_grad = joined(w_grad[:, :256], lax.ppermute(w_grad[:, 256:], ALL, PAIRS["core"]), core, 0)
    down_grad = joined(d_grad[:128], lax.ppermute(d_grad[128:], ALL, PAIRS["core"]), core, 1)
    return input_grad, w_grad[:, :128][None], w_grad[:, 128:][None], down_grad[None]


def solution(mesh):
    rows, deep, wide = P(ALL, None), P("node", None, "blk"), P("node", "blk", None)
    return jax.shard_map(
        on_device,
        mesh=mesh,
        in_specs=(rows, rows, rows, rows, deep, deep, wide),
        out_specs=(rows, deep, deep, wide),
        check_vma=False,
    )
```

```python
import jax
import jax.numpy as jnp
import numpy as np
from jax import lax
from jax.experimental import pallas as pl
from jax.experimental.pallas import tpu as pltpu
from jax.sharding import PartitionSpec as P

ALL = ("node", "blk")
SIZES = (4, 2, 4, 4)
AXIS = {"x": 0, "z": 2, "y": 3}
ORDERS = (("x", "y", "z"), ("y", "z", "x"), ("z", "x", "y"))
PARTS = ((0, 9), (9, 18), (18, 28))
TOK = 14
HALF = 3584
WIDE = HALF + 128
UNIT = 24
WINDOW = 5
TILE = 512
ROWS = 448
BOUNDS = tuple((16 * lo, 16 * hi) for lo, hi in PARTS)
FIRST, SECOND = (1, 3), (3, 1)
OWNERS = ((0, 1, 3, 2), (0, 3, 1, 2))


class Held:
    def __init__(self, value):
        self.value = value


class Link:
    def __init__(self):
        self.sent = []

    def send(self, value, pairs):
        if len(self.sent) >= WINDOW:
            before = self.sent[-WINDOW]
            value, before.value = lax.optimization_barrier((value, before.value))
        self.sent.append(Held(lax.ppermute(value, ALL, pairs)))
        return self.sent[-1]

    def swap(self, value):
        return self.send(value, PAIRS["core"])

    def hop(self, value, axis, turn):
        return self.send(value, PAIRS[axis, turn])

    def gather(self, values, axes, before_second=()):
        first = [self.hop(v, axis, 0) for v, axis in zip(values, axes)]
        pairs = [jnp.concatenate([v, f.value], 0) for v, f in zip(values, first)]
        if before_second:
            after(pairs, before_second)
        second = [self.hop(p, axis, 1) for p, axis in zip(pairs, axes)]
        return [jnp.concatenate([p, s.value], 0) for p, s in zip(pairs, second)]

    def reduce(self, terms, axes):
        size = [t.shape[0] // 4 for t in terms]
        far = [self.hop(t[2 * n :], axis, 1) for t, n, axis in zip(terms, size, axes)]
        first = [self.hop(added(t[n : 2 * n], f.value[n:]), axis, 0) for t, n, f, axis in zip(terms, size, far, axes)]
        return [added(t[:n], f.value[:n], g.value) for t, n, f, g in zip(terms, size, far, first)]


def after(values, held):
    tied = lax.optimization_barrier((tuple(values), tuple(h.value for h in held)))
    values[:] = tied[0]
    for h, value in zip(held, tied[1]):
        h.value = value


def added(*terms):
    total = terms[0].astype(jnp.float32)
    for term in terms[1:]:
        total = total + term.astype(jnp.float32)
    return total.astype(jnp.bfloat16)


def paired(target):
    pairs = []
    for at in np.ndindex(*SIZES):
        pairs.append((int(np.ravel_multi_index(at, SIZES)), int(np.ravel_multi_index(target(at), SIZES))))
    return pairs


def neighbour(axis, by_core):
    def target(at):
        to = list(at)
        to[axis] = to[axis] ^ by_core[at[1]]
        return tuple(to)

    return target


PAIRS = {"core": paired(lambda at: (at[0], 1 - at[1], at[2], at[3]))}
for _name, _axis in AXIS.items():
    PAIRS[_name, 0] = paired(neighbour(_axis, FIRST))
    PAIRS[_name, 1] = paired(neighbour(_axis, SECOND))


def place(core, pick):
    tables = []
    for c in (0, 1):
        rows, width = pick(c)
        table = np.zeros((len(rows), width), np.float32)
        for r, column in enumerate(rows):
            if column >= 0:
                table[r, column] = 1
        tables.append(table)
    return jnp.where(core == 0, jnp.asarray(tables[0], jnp.bfloat16), jnp.asarray(tables[1], jnp.bfloat16))


def move(table, value):
    return jnp.dot(table, value, preferred_element_type=jnp.float32).astype(jnp.bfloat16)


def pick_first(c):
    rows = []
    for lo, hi in PARTS:
        part = []
        for kind in (0, 1):
            for i in range(lo, hi):
                source = 0 if i // TOK == c else 2 * TOK
                part.append(source + kind * TOK + i % TOK)
        rows += part + [-1] * (UNIT - len(part))
    return rows, 4 * TOK


def pick_joined(n, stride):
    def pick(c):
        rows = []
        for kind in (0, 1):
            for j in range(4):
                rows += [OWNERS[c].index(j) * stride + kind * n + i for i in range(n)]
        return rows, 4 * stride

    return pick


def pick_split(n, held, padded):
    def pick(c):
        rows = []
        for q in range(4):
            rows += [OWNERS[c][q] * n + i for i in range(n)] + [-1] * (padded - n)
        return rows, held

    return pick


def pick_last(c):
    rows = []
    for core in (c, 1 - c):
        for t in range(TOK):
            i = core * TOK + t
            p = [p for p in range(3) if PARTS[p][0] <= i < PARTS[p][1]][0]
            rows.append(16 * p + i - PARTS[p][0])
        rows += [-1, -1]
    return rows, 48


def half(value, which, axis):
    size = value.shape[axis] // 2
    return lax.dynamic_slice_in_dim(value, which * size, size, axis)


def joined(own, other, core, axis):
    return jnp.where(core == 0, jnp.concatenate([own, other], axis), jnp.concatenate([other, own], axis))


def dot(a, b, over):
    return lax.dot_general(a, b, (over, ((), ())), preferred_element_type=jnp.float32)


ACROSS = ((1,), (1,))
ALONG = ((1,), (0,))


def params():
    return pltpu.CompilerParams(dimension_semantics=("arbitrary",), vmem_limit_bytes=40 * 1024 * 1024)


def forward_kernel(b0, b1, b2, w_own, w_other, d_own, d_other, sums):
    @pl.when(pl.program_id(0) == 0)
    def _():
        sums[...] = jnp.zeros_like(sums)

    for block, (lo, hi) in zip((b0, b1, b2), BOUNDS):
        n = hi - lo
        x_rows, g_rows = block[:n, :], block[n:, :]
        sums[lo:hi, 0:256] += dot(x_rows, w_own[...], ALONG)
        sums[lo:hi, 256:512] += dot(x_rows, w_other[...], ALONG)
        sums[lo:hi, 512:640] += dot(g_rows, d_own[...], ACROSS)
        sums[lo:hi, 640:768] += dot(g_rows, d_other[...], ACROSS)


def forward(blocks, weights):
    tall = pl.BlockSpec((TILE, 256), lambda i: (i, 0))
    flat = pl.BlockSpec((128, TILE), lambda i: (0, i))
    return pl.pallas_call(
        forward_kernel,
        grid=(HALF // TILE,),
        in_specs=[pl.BlockSpec((b.shape[0], TILE), lambda i: (0, i)) for b in blocks] + [tall, tall, flat, flat],
        out_specs=pl.BlockSpec((ROWS, 768), lambda i: (0, 0)),
        out_shape=jax.ShapeDtypeStruct((ROWS, 768), jnp.float32),
        compiler_params=params(),
        cost_estimate=pl.CostEstimate(flops=2 * ROWS * 768 * HALF, bytes_accessed=14_000_000, transcendentals=0),
    )(*blocks, *weights)


def backward_kernel(mine, arrived, t0, t1, t2, chosen, w_own, w_other, delta, activation, p0, p1, p2, held):
    @pl.when(pl.program_id(0) == 0)
    def _():
        for tail, (lo, hi) in zip((t0, t1, t2), BOUNDS):
            gates = dot(tail[hi - lo :, :], chosen[...], ALONG)
            for e in (0, 1):
                near, far = 256 * e, 256 * (1 - e)
                gate = gates[:, e : e + 1]
                pre_gate = mine[lo:hi, near : near + 128] + arrived[lo:hi, far : far + 128]
                pre_up = mine[lo:hi, near + 128 : near + 256] + arrived[lo:hi, far + 128 : far + 256]
                near, far = 512 + 128 * e, 640 - 128 * e
                act_grad = gate * (mine[lo:hi, near : near + 128] + arrived[lo:hi, far : far + 128])
                sigmoid_gate = jax.nn.sigmoid(pre_gate)
                silu_gate = pre_gate * sigmoid_gate
                gate_delta = act_grad * pre_up * sigmoid_gate * (1.0 + pre_gate * (1.0 - sigmoid_gate))
                held[lo:hi, 256 * e : 256 * e + 128] = gate_delta.astype(jnp.bfloat16)
                held[lo:hi, 256 * e + 128 : 256 * e + 256] = (act_grad * silu_gate).astype(jnp.bfloat16)
                activation[lo:hi, 128 * e : 128 * e + 128] = (gate * (silu_gate * pre_up)).astype(jnp.bfloat16)
        delta[...] = held[...]

    for piece, (lo, hi) in zip((p0, p1, p2), BOUNDS):
        total = dot(held[lo:hi, 0:256], w_own[...], ACROSS) + dot(held[lo:hi, 256:512], w_other[...], ACROSS)
        piece[...] = total.astype(jnp.bfloat16)


def backward(mine, arrived, part, blocks, chosen, weights):
    whole = pl.BlockSpec((ROWS, 768), lambda i: (0, 0))
    tall = pl.BlockSpec((TILE, 256), lambda i: (i, 0))
    sizes = [hi - lo for lo, hi in BOUNDS]
    return pl.pallas_call(
        backward_kernel,
        grid=(HALF // TILE,),
        in_specs=[whole, pl.BlockSpec((ROWS, 768), lambda i: (part, 0))]
        + [pl.BlockSpec((b.shape[0], 128), lambda i: (0, HALF // 128)) for b in blocks]
        + [pl.BlockSpec((128, 128), lambda i: (0, 0)), tall, tall],
        out_specs=[pl.BlockSpec((ROWS, 512), lambda i: (0, 0)), pl.BlockSpec((ROWS, 256), lambda i: (0, 0))]
        + [pl.BlockSpec((n, TILE), lambda i: (0, i)) for n in sizes],
        out_shape=[jax.ShapeDtypeStruct((ROWS, 512), jnp.bfloat16), jax.ShapeDtypeStruct((ROWS, 256), jnp.bfloat16)]
        + [jax.ShapeDtypeStruct((n, HALF), jnp.bfloat16) for n in sizes],
        scratch_shapes=[pltpu.VMEM((ROWS, 512), jnp.bfloat16)],
        compiler_params=params(),
        cost_estimate=pl.CostEstimate(
            flops=2 * ROWS * 512 * HALF, bytes_accessed=12_000_000, transcendentals=ROWS * 256
        ),
    )(mine, arrived, *blocks, chosen, *weights[:2])


def tall_kernel(*refs):
    blocks, deltas, (own, other) = refs[:12], refs[12:16], refs[16:]
    total = jnp.zeros((512, TILE), jnp.float32)
    for q in range(4):
        rows = [b[: hi - lo, :] for b, (lo, hi) in zip(blocks[3 * q : 3 * q + 3], BOUNDS)]
        total = total + dot(deltas[q][...], jnp.concatenate(rows, 0), ALONG)
    total = total.T
    own[...] = total[:, :256].astype(jnp.bfloat16)
    other[...] = total[:, 256:].astype(jnp.bfloat16)


def flat_kernel(*refs):
    blocks, activations, (own, other) = refs[:12], refs[12:16], refs[16:]
    total = jnp.zeros((256, TILE), jnp.float32)
    for q in range(4):
        rows = [b[hi - lo :, :] for b, (lo, hi) in zip(blocks[3 * q : 3 * q + 3], BOUNDS)]
        total = total + dot(activations[q][...], jnp.concatenate(rows, 0), ALONG)
    own[...] = total[:128].astype(jnp.bfloat16)
    other[...] = total[128:].astype(jnp.bfloat16)


def weight_grads(kernel, blocks, turned, shape, block, index):
    parts = [b for four in blocks for b in four]
    width = turned[0].shape[0]
    return pl.pallas_call(
        kernel,
        grid=(HALF // TILE,),
        in_specs=[pl.BlockSpec((b.shape[0], TILE), lambda i: (0, i)) for b in parts]
        + [pl.BlockSpec((width, ROWS), lambda i: (0, 0)) for _ in turned],
        out_specs=[pl.BlockSpec(block, index)] * 2,
        out_shape=[jax.ShapeDtypeStruct(shape, jnp.bfloat16)] * 2,
        compiler_params=params(),
        cost_estimate=pl.CostEstimate(flops=8 * ROWS * width * HALF, bytes_accessed=30_000_000, transcendentals=0),
    )(*parts, *turned)


def on_device(tokens, out_grad, expert_ids, gates, w_gate, w_up, w_down):
    node = lax.axis_index("node")
    core = node % 2
    link = Link()
    sizes = [hi - lo for lo, hi in PARTS]

    onehot = expert_ids[:, :, None] == jnp.arange(8, dtype=jnp.int32)
    gate_sum = jnp.sum(onehot.astype(jnp.float32) * gates.astype(jnp.float32)[:, :, None], axis=1).astype(jnp.bfloat16)
    gate_sum = jnp.pad(jnp.concatenate([jnp.zeros_like(gate_sum), gate_sum], 0), ((0, 0), (0, 120)))
    both = jnp.concatenate([tokens, out_grad], 0)
    other = link.swap(jnp.concatenate([half(both, 1 - core, 1), gate_sum], 1))
    rows = jnp.concatenate([jnp.concatenate([half(both, core, 1), gate_sum], 1), other.value], 0)
    units = move(place(core, pick_first), rows)

    held = link.gather([units[p * UNIT : (p + 1) * UNIT] for p in range(3)], [o[0] for o in ORDERS])
    units = [move(place(core, pick_joined(n, UNIT)), h) for n, h in zip(sizes, held)]

    raw = [w_gate[0], w_up[0], w_down[0]]
    after(raw, [Held(units[0])])
    w_own = jnp.concatenate([half(raw[0], core, 0), half(raw[1], core, 0)], 1)
    w_other = jnp.concatenate([half(raw[0], 1 - core, 0), half(raw[1], 1 - core, 0)], 1)
    d_own, d_other = half(raw[2], core, 1), half(raw[2], 1 - core, 1)
    w_other, d_other = Held(lax.ppermute(w_other, ALL, PAIRS["core"])), Held(lax.ppermute(d_other, ALL, PAIRS["core"]))
    held = link.gather(units, [o[1] for o in ORDERS], [w_other, d_other])
    units = [move(place(core, pick_joined(4 * n, 8 * n)), h) for n, h in zip(sizes, held)]
    weights = (w_own, w_other.value, d_own, d_other.value)

    axes = [o[2] for o in ORDERS]
    chosen = jnp.arange(128)[None, :] == jnp.array([0, 1])[:, None]
    wanted = jnp.stack([node, node + 1 - 2 * core])
    chosen = jnp.sum(
        (jnp.arange(128)[:, None, None] == wanted[None, :, None]) & chosen[None], axis=1
    ).astype(jnp.bfloat16)

    def values(q):
        return [b.value for b in blocks[q]]

    blocks = [[Held(u) for u in units], None, None, None]
    blocks[1] = [link.hop(b.value, axis, 0) for b, axis in zip(blocks[0], axes)]
    blocks[2] = [link.hop(b.value, axis, 1) for b, axis in zip(blocks[0], axes)]
    early = values(0)
    after(early, [blocks[1][2]])
    sums = [forward(early, weights), None, None, None]
    arrived = link.swap(sums[0])
    blocks[3] = [link.hop(b.value, axis, 1) for b, axis in zip(blocks[1], axes)]
    sums[1], sums[2] = forward(values(1), weights), forward(values(2), weights)
    both = link.swap(jnp.concatenate([sums[2], sums[1]], 0))
    done = [backward(sums[0], arrived.value, 0, values(0), chosen, weights), None, None, None]
    done[2] = backward(sums[2], both.value, 1, values(2), chosen, weights)
    second = [link.hop(t, axis, 1) for t, axis in zip(done[2][2:], axes)]
    sums[3] = forward(values(3), weights)
    arrived = link.swap(sums[3])
    done[1] = backward(sums[1], both.value, 0, values(1), chosen, weights)
    done[3] = backward(sums[3], arrived.value, 0, values(3), chosen, weights)
    far = [link.hop(t, axis, 1) for t, axis in zip(done[3][2:], axes)]
    first = [link.hop(added(t, f.value), axis, 0) for t, f, axis in zip(done[1][2:], far, axes)]
    totals = [added(t, s.value, f.value) for t, s, f in zip(done[0][2:], second, first)]

    terms = [move(place(core, pick_split(4 * n, 16 * n, 40)), t) for n, t in zip(sizes, totals)]
    totals = link.reduce(terms, [o[1] for o in ORDERS])
    terms = [move(place(core, pick_split(n, 40, 16)), t) for n, t in zip(sizes, totals)]
    totals = link.reduce(terms, [o[0] for o in ORDERS])
    finished = move(place(core, pick_last), jnp.concatenate(totals, 0))
    arrived = link.swap(finished[16 : 16 + TOK])
    input_grad = joined(finished[:TOK], arrived.value, core, 1)

    every = [values(q) for q in range(4)]
    d_grad = weight_grads(
        flat_kernel, every, [d[1].T for d in done], (128, HALF), (128, TILE), lambda i: (0, i)
    )
    w_grad = weight_grads(
        tall_kernel, every, [d[0].T for d in done], (HALF, 256), (TILE, 256), lambda i: (i, 0)
    )
    w_grad = joined(w_grad[0], lax.ppermute(w_grad[1], ALL, PAIRS["core"]), core, 0)
    down_grad = joined(d_grad[0], lax.ppermute(d_grad[1], ALL, PAIRS["core"]), core, 1)
    return input_grad, w_grad[:, :128][None], w_grad[:, 128:][None], down_grad[None]


def solution(mesh):
    rows, deep, wide = P(ALL, None), P("node", None, "blk"), P("node", "blk", None)
    return jax.shard_map(
        on_device,
        mesh=mesh,
        in_specs=(rows, rows, rows, rows, deep, deep, wide),
        out_specs=(rows, deep, deep, wide),
        check_vma=False,
    )
```

```python
import jax
import jax.numpy as jnp
import numpy as np
from jax import lax
from jax.experimental import pallas as pl
from jax.experimental.pallas import tpu as pltpu
from jax.sharding import PartitionSpec as P

ALL = ("node", "blk")
SIZES = (4, 2, 4, 4)
AXIS = {"x": 0, "z": 2, "y": 3}
ORDERS = (("x", "y", "z"), ("y", "z", "x"), ("z", "x", "y"))
PARTS = ((0, 9), (9, 18), (18, 28))
TOK = 14
HALF = 3584
WIDE = HALF + 128
UNIT = 24
TILE = 1792
GRAD_TILE = 896
ROWS = 448
BOUNDS = tuple((16 * lo, 16 * hi) for lo, hi in PARTS)
FIRST, SECOND = (1, 3), (3, 1)
OWNERS = ((0, 1, 3, 2), (0, 3, 1, 2))


def swap(value):
    return lax.ppermute(value, ALL, PAIRS["core"])


def hops(values, axes, turn):
    return [lax.ppermute(v, ALL, PAIRS[axis, turn]) for v, axis in zip(values, axes)]


def stage(*values):
    return lax.optimization_barrier(values)


def added(*terms):
    total = terms[0].astype(jnp.float32)
    for term in terms[1:]:
        total = total + term.astype(jnp.float32)
    return total.astype(jnp.bfloat16)


def paired(target):
    pairs = []
    for at in np.ndindex(*SIZES):
        pairs.append((int(np.ravel_multi_index(at, SIZES)), int(np.ravel_multi_index(target(at), SIZES))))
    return pairs


def neighbour(axis, by_core):
    def target(at):
        to = list(at)
        to[axis] = to[axis] ^ by_core[at[1]]
        return tuple(to)

    return target


PAIRS = {"core": paired(lambda at: (at[0], 1 - at[1], at[2], at[3]))}
for _name, _axis in AXIS.items():
    PAIRS[_name, 0] = paired(neighbour(_axis, FIRST))
    PAIRS[_name, 1] = paired(neighbour(_axis, SECOND))


def place(core, pick):
    tables = []
    for c in (0, 1):
        rows, width = pick(c)
        table = np.zeros((len(rows), width), np.float32)
        for r, column in enumerate(rows):
            if column >= 0:
                table[r, column] = 1
        tables.append(table)
    return jnp.where(core == 0, jnp.asarray(tables[0], jnp.bfloat16), jnp.asarray(tables[1], jnp.bfloat16))


def move(table, value):
    return jnp.dot(table, value, preferred_element_type=jnp.float32).astype(jnp.bfloat16)


def pick_first(c):
    rows = []
    for lo, hi in PARTS:
        part = []
        for kind in (0, 1):
            for i in range(lo, hi):
                source = 0 if i // TOK == c else 2 * TOK
                part.append(source + kind * TOK + i % TOK)
        rows += part + [-1] * (UNIT - len(part))
    return rows, 4 * TOK


def pick_joined(n, stride, total):
    def pick(c):
        rows = []
        for kind in (0, 1):
            for j in range(4):
                rows += [OWNERS[c].index(j) * stride + kind * n + i for i in range(n)]
        return rows + [-1] * (total - len(rows)), 4 * stride

    return pick


def pick_split(n, held, padded, blocks):
    def pick(c):
        rows = []
        for q in blocks:
            rows += [OWNERS[c][q] * n + i for i in range(n)] + [-1] * (padded - n)
        return rows, held

    return pick


def pick_last(c):
    rows = []
    for core in (c, 1 - c):
        for t in range(TOK):
            i = core * TOK + t
            p = [p for p in range(3) if PARTS[p][0] <= i < PARTS[p][1]][0]
            rows.append(16 * p + i - PARTS[p][0])
        rows += [-1, -1]
    return rows, 48


def half(value, which, axis):
    size = value.shape[axis] // 2
    return lax.dynamic_slice_in_dim(value, which * size, size, axis)


def joined(own, other, core, axis):
    return jnp.where(core == 0, jnp.concatenate([own, other], axis), jnp.concatenate([other, own], axis))


def dot(a, b, over):
    return lax.dot_general(a, b, (over, ((), ())), preferred_element_type=jnp.float32)


COST = pl.CostEstimate(flops=1, bytes_accessed=1, transcendentals=0)
ACROSS = ((1,), (1,))
ALONG = ((1,), (0,))
DOWN = ((0,), (0,))


def params():
    return pltpu.CompilerParams(dimension_semantics=("arbitrary",), vmem_limit_bytes=60 * 1024 * 1024)


def x_rows(blocks):
    return jnp.concatenate([b[: hi - lo, :] for b, (lo, hi) in zip(blocks, BOUNDS)], 0)


def g_rows(blocks):
    return jnp.concatenate([b[hi - lo :, :] for b, (lo, hi) in zip(blocks, BOUNDS)], 0)


def forward_kernel(b0, b1, b2, w_own, w_other, d_own, d_other, sums):
    pre = dot(x_rows((b0, b1, b2)), jnp.concatenate([w_own[...], w_other[...]], 1), ALONG)
    act = dot(g_rows((b0, b1, b2)), jnp.concatenate([d_own[...], d_other[...]], 0), ACROSS)

    @pl.when(pl.program_id(0) == 0)
    def _():
        sums[:, :512] = pre
        sums[:, 512:] = act

    @pl.when(pl.program_id(0) > 0)
    def _():
        sums[:, :512] += pre
        sums[:, 512:] += act


def forward(blocks, weights):
    tall = pl.BlockSpec((TILE, 256), lambda i: (i, 0))
    flat = pl.BlockSpec((128, TILE), lambda i: (0, i))
    return pl.pallas_call(
        forward_kernel,
        grid=(HALF // TILE,),
        in_specs=[pl.BlockSpec((b.shape[0], TILE), lambda i: (0, i)) for b in blocks] + [tall, tall, flat, flat],
        out_specs=pl.BlockSpec((ROWS, 768), lambda i: (0, 0)),
        out_shape=jax.ShapeDtypeStruct((ROWS, 768), jnp.float32),
        compiler_params=params(),
        cost_estimate=COST,
    )(*blocks, *weights)


def backward_kernel(mine, arrived, t0, t1, t2, chosen, w_own, w_other, delta, activation, p0, p1, p2, held):
    @pl.when(pl.program_id(0) == 0)
    def _():
        for tail, (lo, hi) in zip((t0, t1, t2), BOUNDS):
            gates = dot(tail[hi - lo :, :], chosen[...], ALONG)
            for e in (0, 1):
                near, far = 256 * e, 256 * (1 - e)
                gate = gates[:, e : e + 1]
                pre_gate = mine[lo:hi, near : near + 128] + arrived[lo:hi, far : far + 128]
                pre_up = mine[lo:hi, near + 128 : near + 256] + arrived[lo:hi, far + 128 : far + 256]
                near, far = 512 + 128 * e, 640 - 128 * e
                act_grad = gate * (mine[lo:hi, near : near + 128] + arrived[lo:hi, far : far + 128])
                sigmoid_gate = jax.nn.sigmoid(pre_gate)
                silu_gate = pre_gate * sigmoid_gate
                gate_delta = act_grad * pre_up * sigmoid_gate * (1.0 + pre_gate * (1.0 - sigmoid_gate))
                held[lo:hi, 256 * e : 256 * e + 128] = gate_delta.astype(jnp.bfloat16)
                held[lo:hi, 256 * e + 128 : 256 * e + 256] = (act_grad * silu_gate).astype(jnp.bfloat16)
                activation[lo:hi, 128 * e : 128 * e + 128] = (gate * (silu_gate * pre_up)).astype(jnp.bfloat16)
        delta[...] = held[...]

    total = dot(held[...], jnp.concatenate([w_own[...], w_other[...]], 1), ACROSS).astype(jnp.bfloat16)
    for piece, (lo, hi) in zip((p0, p1, p2), BOUNDS):
        piece[...] = total[lo:hi]


def backward(mine, arrived, blocks, chosen, weights):
    whole = pl.BlockSpec((ROWS, 768), lambda i: (0, 0))
    tall = pl.BlockSpec((TILE, 256), lambda i: (i, 0))
    sizes = [hi - lo for lo, hi in BOUNDS]
    return pl.pallas_call(
        backward_kernel,
        grid=(HALF // TILE,),
        in_specs=[whole, whole]
        + [pl.BlockSpec((b.shape[0], 128), lambda i: (0, HALF // 128)) for b in blocks]
        + [pl.BlockSpec((128, 128), lambda i: (0, 0)), tall, tall],
        out_specs=[pl.BlockSpec((ROWS, 512), lambda i: (0, 0)), pl.BlockSpec((ROWS, 256), lambda i: (0, 0))]
        + [pl.BlockSpec((n, TILE), lambda i: (0, i)) for n in sizes],
        out_shape=[jax.ShapeDtypeStruct((ROWS, 512), jnp.bfloat16), jax.ShapeDtypeStruct((ROWS, 256), jnp.bfloat16)]
        + [jax.ShapeDtypeStruct((n, HALF), jnp.bfloat16) for n in sizes],
        scratch_shapes=[pltpu.VMEM((ROWS, 512), jnp.bfloat16)],
        compiler_params=params(),
        cost_estimate=COST,
    )(mine, arrived, *blocks, chosen, *weights[:2])


def rows_of(refs):
    return jnp.concatenate([r[...] for r in refs], 0)


def tall_kernel(*refs):
    blocks, deltas, (own, other) = refs[:12], refs[12:16], refs[16:]
    total = dot(rows_of(blocks), rows_of(deltas), DOWN)
    own[...] = total[:, :256].astype(jnp.bfloat16)
    other[...] = total[:, 256:].astype(jnp.bfloat16)


def flat_kernel(*refs):
    blocks, activations, (own, other) = refs[:12], refs[12:16], refs[16:]
    total = dot(rows_of(activations), rows_of(blocks), DOWN)
    own[...] = total[:128].astype(jnp.bfloat16)
    other[...] = total[128:].astype(jnp.bfloat16)


def weight_grads(kernel, blocks, hidden, kind, shape, block, index):
    parts = [b for four in blocks for b in four]
    width = hidden[0].shape[1]
    return pl.pallas_call(
        kernel,
        grid=(HALF // GRAD_TILE,),
        in_specs=[pl.BlockSpec((b.shape[0] // 2, GRAD_TILE), lambda i: (kind, i)) for b in parts]
        + [pl.BlockSpec((ROWS, width), lambda i: (0, 0)) for _ in hidden],
        out_specs=[pl.BlockSpec(block, index)] * 2,
        out_shape=[jax.ShapeDtypeStruct(shape, jnp.bfloat16)] * 2,
        compiler_params=params(),
        cost_estimate=COST,
    )(*parts, *hidden)


def tall_grads(blocks, deltas):
    return weight_grads(tall_kernel, blocks, deltas, 0, (HALF, 256), (GRAD_TILE, 256), lambda i: (i, 0))


def flat_grads(blocks, activations):
    return weight_grads(flat_kernel, blocks, activations, 1, (128, HALF), (128, GRAD_TILE), lambda i: (0, i))


def on_device(tokens, out_grad, expert_ids, gates, w_gate, w_up, w_down):
    node = lax.axis_index("node")
    core = node % 2
    sizes = [hi - lo for lo, hi in PARTS]
    small, middle, large = ([o[i] for o in ORDERS] for i in range(3))

    onehot = expert_ids[:, :, None] == jnp.arange(8, dtype=jnp.int32)
    gate_sum = jnp.sum(onehot.astype(jnp.float32) * gates.astype(jnp.float32)[:, :, None], axis=1).astype(jnp.bfloat16)
    gate_sum = jnp.pad(jnp.concatenate([jnp.zeros_like(gate_sum), gate_sum], 0), ((0, 0), (0, 120)))
    both = jnp.concatenate([tokens, out_grad], 0)
    other = swap(jnp.concatenate([half(both, 1 - core, 1), gate_sum], 1))
    rows = jnp.concatenate([jnp.concatenate([half(both, core, 1), gate_sum], 1), other], 0)
    units = move(place(core, pick_first), rows)
    units = [units[p * UNIT : (p + 1) * UNIT] for p in range(3)]

    def gathered(units, axes, beside):
        first, beside = stage(hops(units, axes, 0), beside)
        pairs = [jnp.concatenate([u, f], 0) for u, f in zip(units, first)]
        second = hops(pairs, axes, 1)
        return [jnp.concatenate([p, s], 0) for p, s in zip(pairs, second)], beside

    units, raw = stage(units, (w_gate[0], w_up[0], w_down[0]))
    w_own = jnp.concatenate([half(raw[0], core, 0), half(raw[1], core, 0)], 1)
    w_other = jnp.concatenate([half(raw[0], 1 - core, 0), half(raw[1], 1 - core, 0)], 1)
    d_own, d_other = half(raw[2], core, 1), half(raw[2], 1 - core, 1)
    held, (w_own, w_other, d_own, d_other) = gathered(units, small, [w_own, w_other, d_own, d_other])
    units = [move(place(core, pick_joined(n, UNIT, 80)), h) for n, h in zip(sizes, held)]
    held, (w_other, d_other) = gathered(units, middle, [swap(w_other), swap(d_other)])
    held, w_other, d_other = stage(held, w_other, d_other)
    units = [move(place(core, pick_joined(4 * n, 80, 32 * n)), h) for n, h in zip(sizes, held)]
    weights = (w_own, w_other, d_own, d_other)

    wanted = jnp.stack([node, node + 1 - 2 * core])
    chosen = jnp.arange(128)[None, :] == jnp.array([0, 1])[:, None]
    chosen = jnp.sum(
        (jnp.arange(128)[:, None, None] == wanted[None, :, None]) & chosen[None], axis=1
    ).astype(jnp.bfloat16)

    own, sums, arrived, done = units, [None] * 4, [None] * 4, [None] * 4
    first = hops(own, large, 0)
    own, sums[0] = stage(own, forward(own, weights))
    second = hops(own, large, 1)
    done[0] = backward(sums[0], swap(sums[0]), own, chosen, weights)
    first, done[0] = stage(first, done[0])
    far = hops(first, large, 1)
    first, second = stage(first, second)
    sums[1], sums[2] = forward(first, weights), forward(second, weights)
    arrived[2], arrived[1] = stage(swap(sums[1]), swap(sums[2]))
    done[2] = backward(sums[2], arrived[2], second, chosen, weights)
    done[1] = backward(sums[1], arrived[1], first, chosen, weights)
    far, done[1], done[2] = stage(far, done[1], done[2])

    from_second = hops(done[2][2:], large, 1)
    sums[3] = forward(far, weights)
    done[3] = backward(sums[3], swap(sums[3]), far, chosen, weights)
    from_second, done[3] = stage(from_second, done[3])

    every = [own, first, second, far]
    from_far, d_grad = stage(hops(done[3][2:], large, 1), flat_grads(every, [d[1] for d in done]))
    totals = [added(t, f) for t, f in zip(done[1][2:], from_far)]
    from_first, w_grad, d_arrived = stage(hops(totals, large, 0), tall_grads(every, [d[0] for d in done]), swap(d_grad[1]))
    totals = [added(t, s, f) for t, s, f in zip(done[0][2:], from_second, from_first)]

    def reduced(totals, axes, blocks, held, padded, beside):
        outer = [move(place(core, pick_split(n, h, padded, (2, 3))), t) for n, h, t in zip(blocks, held, totals)]
        far = hops(outer, axes, 1)
        inner = [move(place(core, pick_split(n, h, padded, (0, 1))), t) for n, h, t in zip(blocks, held, totals)]
        middle = [added(t[padded:], f[padded:]) for t, f in zip(inner, far)]
        first, beside = stage(hops(middle, axes, 0), beside)
        return [added(t[:padded], f[:padded], g) for t, f, g in zip(inner, far, first)], beside

    totals, w_arrived = reduced(
        totals, middle, [4 * n for n in sizes], [16 * n for n in sizes], 40, swap(w_grad[1])
    )
    w_grad = joined(w_grad[0], w_arrived, core, 0)
    down_grad = joined(d_grad[0], d_arrived, core, 1)
    totals, (w_grad, down_grad) = reduced(totals, small, sizes, [40] * 3, 16, (w_grad, down_grad))
    finished = move(place(core, pick_last), jnp.concatenate(totals, 0))
    arrived = swap(finished[16 : 16 + TOK])
    input_grad = joined(finished[:TOK], arrived, core, 1)
    return input_grad, w_grad[:, :128][None], w_grad[:, 128:][None], down_grad[None]


def solution(mesh):
    rows, deep, wide = P(ALL, None), P("node", None, "blk"), P("node", "blk", None)
    return jax.shard_map(
        on_device,
        mesh=mesh,
        in_specs=(rows, rows, rows, rows, deep, deep, wide),
        out_specs=(rows, deep, deep, wide),
        check_vma=False,
    )
```

```python
import jax
import jax.numpy as jnp
import numpy as np
from jax import lax
from jax.experimental import pallas as pl
from jax.experimental.pallas import tpu as pltpu
from jax.sharding import PartitionSpec as P

ALL = ("node", "blk")
SIZES = (4, 2, 4, 4)
AXIS = {"x": 0, "z": 2, "y": 3}
ORDERS = (("x", "y", "z"), ("y", "z", "x"), ("z", "x", "y"))
PARTS = ((0, 9), (9, 18), (18, 28))
TOK = 14
HALF = 3584
WIDE = HALF + 128
UNIT = 24
TILE = 1792
GRAD_TILE = 896
ROWS = 448
BOUNDS = tuple((16 * lo, 16 * hi) for lo, hi in PARTS)
FIRST, SECOND = (1, 3), (3, 1)
OWNERS = ((0, 1, 3, 2), (0, 3, 1, 2))


def swap(value):
    return lax.ppermute(value, ALL, PAIRS["core"])


def hops(values, axes, turn):
    return [lax.ppermute(v, ALL, PAIRS[axis, turn]) for v, axis in zip(values, axes)]


def stage(*values):
    return lax.optimization_barrier(values)


def added(*terms):
    total = terms[0].astype(jnp.float32)
    for term in terms[1:]:
        total = total + term.astype(jnp.float32)
    return total.astype(jnp.bfloat16)


def paired(target):
    pairs = []
    for at in np.ndindex(*SIZES):
        pairs.append((int(np.ravel_multi_index(at, SIZES)), int(np.ravel_multi_index(target(at), SIZES))))
    return pairs


def neighbour(axis, by_core):
    def target(at):
        to = list(at)
        to[axis] = to[axis] ^ by_core[at[1]]
        return tuple(to)

    return target


PAIRS = {"core": paired(lambda at: (at[0], 1 - at[1], at[2], at[3]))}
for _name, _axis in AXIS.items():
    PAIRS[_name, 0] = paired(neighbour(_axis, FIRST))
    PAIRS[_name, 1] = paired(neighbour(_axis, SECOND))


def place(core, pick):
    tables = []
    for c in (0, 1):
        rows, width = pick(c)
        table = np.zeros((len(rows), width), np.float32)
        for r, column in enumerate(rows):
            if column >= 0:
                table[r, column] = 1
        tables.append(table)
    return jnp.where(core == 0, jnp.asarray(tables[0], jnp.bfloat16), jnp.asarray(tables[1], jnp.bfloat16))


def move(table, value):
    return jnp.dot(table, value, preferred_element_type=jnp.float32).astype(jnp.bfloat16)


def pick_first(c):
    rows = []
    for lo, hi in PARTS:
        part = []
        for kind in (0, 1):
            for i in range(lo, hi):
                source = 0 if i // TOK == c else 2 * TOK
                part.append(source + kind * TOK + i % TOK)
        rows += part + [-1] * (UNIT - len(part))
    return rows, 4 * TOK


def pick_joined(n, stride, total):
    def pick(c):
        rows = []
        for kind in (0, 1):
            for j in range(4):
                rows += [OWNERS[c].index(j) * stride + kind * n + i for i in range(n)]
        return rows + [-1] * (total - len(rows)), 4 * stride

    return pick


def pick_split(n, held, padded, blocks):
    def pick(c):
        rows = []
        for q in blocks:
            rows += [OWNERS[c][q] * n + i for i in range(n)] + [-1] * (padded - n)
        return rows, held

    return pick


def pick_last(c):
    rows = []
    for core in (c, 1 - c):
        for t in range(TOK):
            i = core * TOK + t
            p = [p for p in range(3) if PARTS[p][0] <= i < PARTS[p][1]][0]
            rows.append(16 * p + i - PARTS[p][0])
        rows += [-1, -1]
    return rows, 48


def half(value, which, axis):
    size = value.shape[axis] // 2
    return lax.dynamic_slice_in_dim(value, which * size, size, axis)


def joined(own, other, core, axis):
    return jnp.where(core == 0, jnp.concatenate([own, other], axis), jnp.concatenate([other, own], axis))


def dot(a, b, over):
    return lax.dot_general(a, b, (over, ((), ())), preferred_element_type=jnp.float32)


COST = pl.CostEstimate(flops=1, bytes_accessed=1, transcendentals=0)
ACROSS = ((1,), (1,))
ALONG = ((1,), (0,))
DOWN = ((0,), (0,))


def params():
    return pltpu.CompilerParams(dimension_semantics=("arbitrary",), vmem_limit_bytes=60 * 1024 * 1024)


def x_rows(blocks):
    return jnp.concatenate([b[: hi - lo, :] for b, (lo, hi) in zip(blocks, BOUNDS)], 0)


def g_rows(blocks):
    return jnp.concatenate([b[hi - lo :, :] for b, (lo, hi) in zip(blocks, BOUNDS)], 0)


def forward_kernel(b0, b1, b2, w_own, w_other, d_own, d_other, sums, sent):
    pre = dot(x_rows((b0, b1, b2)), jnp.concatenate([w_own[...], w_other[...]], 1), ALONG)
    act = dot(g_rows((b0, b1, b2)), jnp.concatenate([d_own[...], d_other[...]], 0), ACROSS)

    @pl.when(pl.program_id(0) == 0)
    def _():
        sums[:, :512] = pre
        sums[:, 512:] = act

    @pl.when(pl.program_id(0) > 0)
    def _():
        sums[:, :512] += pre
        sums[:, 512:] += act
        sent[...] = sums[...].astype(jnp.bfloat16)


def forward(blocks, weights):
    tall = pl.BlockSpec((TILE, 256), lambda i: (i, 0))
    flat = pl.BlockSpec((128, TILE), lambda i: (0, i))
    return pl.pallas_call(
        forward_kernel,
        grid=(HALF // TILE,),
        in_specs=[pl.BlockSpec((b.shape[0], TILE), lambda i: (0, i)) for b in blocks] + [tall, tall, flat, flat],
        out_specs=[pl.BlockSpec((ROWS, 768), lambda i: (0, 0))] * 2,
        out_shape=[jax.ShapeDtypeStruct((ROWS, 768), t) for t in (jnp.float32, jnp.bfloat16)],
        compiler_params=params(),
        cost_estimate=COST,
    )(*blocks, *weights)


def backward_kernel(mine, arrived, t0, t1, t2, chosen, w_own, w_other, delta, activation, p0, p1, p2, held):
    @pl.when(pl.program_id(0) == 0)
    def _():
        for tail, (lo, hi) in zip((t0, t1, t2), BOUNDS):
            gates = dot(tail[hi - lo :, :], chosen[...], ALONG)
            for e in (0, 1):
                near, far = 256 * e, 256 * (1 - e)
                gate = gates[:, e : e + 1]
                pre_gate = mine[lo:hi, near : near + 128] + arrived[lo:hi, far : far + 128]
                pre_up = mine[lo:hi, near + 128 : near + 256] + arrived[lo:hi, far + 128 : far + 256]
                near, far = 512 + 128 * e, 640 - 128 * e
                act_grad = gate * (mine[lo:hi, near : near + 128] + arrived[lo:hi, far : far + 128])
                sigmoid_gate = jax.nn.sigmoid(pre_gate)
                silu_gate = pre_gate * sigmoid_gate
                gate_delta = act_grad * pre_up * sigmoid_gate * (1.0 + pre_gate * (1.0 - sigmoid_gate))
                held[lo:hi, 256 * e : 256 * e + 128] = gate_delta.astype(jnp.bfloat16)
                held[lo:hi, 256 * e + 128 : 256 * e + 256] = (act_grad * silu_gate).astype(jnp.bfloat16)
                activation[lo:hi, 128 * e : 128 * e + 128] = (gate * (silu_gate * pre_up)).astype(jnp.bfloat16)
        delta[...] = held[...]

    total = dot(held[...], jnp.concatenate([w_own[...], w_other[...]], 1), ACROSS).astype(jnp.bfloat16)
    for piece, (lo, hi) in zip((p0, p1, p2), BOUNDS):
        piece[...] = total[lo:hi]


def backward(mine, arrived, blocks, chosen, weights):
    whole = pl.BlockSpec((ROWS, 768), lambda i: (0, 0))
    tall = pl.BlockSpec((TILE, 256), lambda i: (i, 0))
    sizes = [hi - lo for lo, hi in BOUNDS]
    return pl.pallas_call(
        backward_kernel,
        grid=(HALF // TILE,),
        in_specs=[whole, whole]
        + [pl.BlockSpec((b.shape[0], 128), lambda i: (0, HALF // 128)) for b in blocks]
        + [pl.BlockSpec((128, 128), lambda i: (0, 0)), tall, tall],
        out_specs=[pl.BlockSpec((ROWS, 512), lambda i: (0, 0)), pl.BlockSpec((ROWS, 256), lambda i: (0, 0))]
        + [pl.BlockSpec((n, TILE), lambda i: (0, i)) for n in sizes],
        out_shape=[jax.ShapeDtypeStruct((ROWS, 512), jnp.bfloat16), jax.ShapeDtypeStruct((ROWS, 256), jnp.bfloat16)]
        + [jax.ShapeDtypeStruct((n, HALF), jnp.bfloat16) for n in sizes],
        scratch_shapes=[pltpu.VMEM((ROWS, 512), jnp.bfloat16)],
        compiler_params=params(),
        cost_estimate=COST,
    )(mine, arrived, *blocks, chosen, *weights[:2])


def rows_of(refs):
    return jnp.concatenate([r[...] for r in refs], 0)


def tall_kernel(*refs):
    blocks, deltas, (own, other) = refs[:12], refs[12:16], refs[16:]
    total = dot(rows_of(blocks), rows_of(deltas), DOWN)
    own[...] = total[:, :256].astype(jnp.bfloat16)
    other[...] = total[:, 256:].astype(jnp.bfloat16)


def flat_kernel(*refs):
    blocks, activations, (own, other) = refs[:12], refs[12:16], refs[16:]
    total = dot(rows_of(activations), rows_of(blocks), DOWN)
    own[...] = total[:128].astype(jnp.bfloat16)
    other[...] = total[128:].astype(jnp.bfloat16)


def weight_grads(kernel, blocks, hidden, kind, shape, block, index):
    parts = [b for four in blocks for b in four]
    width = hidden[0].shape[1]
    return pl.pallas_call(
        kernel,
        grid=(HALF // GRAD_TILE,),
        in_specs=[pl.BlockSpec((b.shape[0] // 2, GRAD_TILE), lambda i: (kind, i)) for b in parts]
        + [pl.BlockSpec((ROWS, width), lambda i: (0, 0)) for _ in hidden],
        out_specs=[pl.BlockSpec(block, index)] * 2,
        out_shape=[jax.ShapeDtypeStruct(shape, jnp.bfloat16)] * 2,
        compiler_params=params(),
        cost_estimate=COST,
    )(*parts, *hidden)


def tall_grads(blocks, deltas):
    return weight_grads(tall_kernel, blocks, deltas, 0, (HALF, 256), (GRAD_TILE, 256), lambda i: (i, 0))


def flat_grads(blocks, activations):
    return weight_grads(flat_kernel, blocks, activations, 1, (128, HALF), (128, GRAD_TILE), lambda i: (0, i))


def on_device(tokens, out_grad, expert_ids, gates, w_gate, w_up, w_down):
    node = lax.axis_index("node")
    core = node % 2
    sizes = [hi - lo for lo, hi in PARTS]
    small, middle, large = ([o[i] for o in ORDERS] for i in range(3))

    onehot = expert_ids[:, :, None] == jnp.arange(8, dtype=jnp.int32)
    gate_sum = jnp.sum(onehot.astype(jnp.float32) * gates.astype(jnp.float32)[:, :, None], axis=1).astype(jnp.bfloat16)
    gate_sum = jnp.pad(jnp.concatenate([jnp.zeros_like(gate_sum), gate_sum], 0), ((0, 0), (0, 120)))
    both = jnp.concatenate([tokens, out_grad], 0)
    other = swap(jnp.concatenate([half(both, 1 - core, 1), gate_sum], 1))
    rows = jnp.concatenate([jnp.concatenate([half(both, core, 1), gate_sum], 1), other], 0)
    units = move(place(core, pick_first), rows)
    units = [units[p * UNIT : (p + 1) * UNIT] for p in range(3)]

    def gathered(units, axes, beside):
        first = hops(units, axes, 0)
        first[0], beside = stage(first[0], beside)
        pairs = [jnp.concatenate([u, f], 0) for u, f in zip(units, first)]
        return pairs, hops(pairs, axes, 1), beside

    units, raw = stage(units, (w_gate[0], w_up[0], w_down[0]))
    w_own = jnp.concatenate([half(raw[0], core, 0), half(raw[1], core, 0)], 1)
    w_other = jnp.concatenate([half(raw[0], 1 - core, 0), half(raw[1], 1 - core, 0)], 1)
    d_own, d_other = half(raw[2], core, 1), half(raw[2], 1 - core, 1)
    pairs, others, (w_own, w_other, d_own, d_other) = gathered(units, small, [w_own, w_other, d_own, d_other])
    units = [
        move(place(core, pick_joined(n, UNIT, 80)), jnp.concatenate([p, s], 0)) for n, p, s in zip(sizes, pairs, others)
    ]
    pairs, others, (w_other, d_other) = gathered(units, middle, [w_other, d_other])
    w_other, d_other = swap(w_other), swap(d_other)
    units = [
        move(place(core, pick_joined(4 * n, 80, 32 * n)), jnp.concatenate([p, s], 0))
        for n, p, s in zip(sizes, pairs, others)
    ]
    weights = (w_own, w_other, d_own, d_other)

    wanted = jnp.stack([node, node + 1 - 2 * core])
    chosen = jnp.arange(128)[None, :] == jnp.array([0, 1])[:, None]
    chosen = jnp.sum(
        (jnp.arange(128)[:, None, None] == wanted[None, :, None]) & chosen[None], axis=1
    ).astype(jnp.bfloat16)

    def paced(values, behind):
        pairs = [stage(v, b) for v, b in zip(values, behind)]
        return [p[0] for p in pairs], [p[1] for p in pairs]

    own, sums, done = units, [None] * 4, [None] * 4
    first = hops(own, large, 0)
    sums[0] = forward(own, weights)
    done[0] = backward(sums[0][0], swap(sums[0][1]), own, chosen, weights)
    own, done[0] = stage(own, done[0])
    own, first = paced(own, first)

    second, sums[1] = hops(own, large, 1), forward(first, weights)
    arrived = swap(sums[1][1])
    first, sums[1], arrived = stage(first, sums[1], arrived)
    first, second = paced(first, second)

    far, sums[2] = hops(first, large, 1), forward(second, weights)
    done[2] = backward(sums[2][0], arrived, second, chosen, weights)
    done[1] = backward(sums[1][0], swap(sums[2][1]), first, chosen, weights)
    done[2], done[1] = stage(done[2], done[1])
    pieces, far = paced(done[2][2:], far)

    from_second, sums[3] = hops(pieces, large, 1), forward(far, weights)
    done[3] = backward(sums[3][0], swap(sums[3][1]), far, chosen, weights)
    from_second, done[3] = stage(from_second, done[3])

    every = [own, first, second, far]
    from_far, d_grad = stage(hops(done[3][2:], large, 1), flat_grads(every, [d[1] for d in done]))
    totals = [added(t, f) for t, f in zip(done[1][2:], from_far)]
    from_first, w_grad, d_arrived = stage(hops(totals, large, 0), tall_grads(every, [d[0] for d in done]), swap(d_grad[1]))
    totals = [added(t, s, f) for t, s, f in zip(done[0][2:], from_second, from_first)]

    def reduced(totals, axes, blocks, held, padded, beside):
        outer = [move(place(core, pick_split(n, h, padded, (2, 3))), t) for n, h, t in zip(blocks, held, totals)]
        far = hops(outer, axes, 1)
        inner = [move(place(core, pick_split(n, h, padded, (0, 1))), t) for n, h, t in zip(blocks, held, totals)]
        middle = [added(t[padded:], f[padded:]) for t, f in zip(inner, far)]
        first, beside = stage(hops(middle, axes, 0), beside)
        return [added(t[:padded], f[:padded], g) for t, f, g in zip(inner, far, first)], beside

    totals, w_arrived = reduced(
        totals, middle, [4 * n for n in sizes], [16 * n for n in sizes], 40, swap(w_grad[1])
    )
    w_grad = joined(w_grad[0], w_arrived, core, 0)
    down_grad = joined(d_grad[0], d_arrived, core, 1)
    totals, (w_grad, down_grad) = reduced(totals, small, sizes, [40] * 3, 16, (w_grad, down_grad))
    finished = move(place(core, pick_last), jnp.concatenate(totals, 0))
    arrived = swap(finished[16 : 16 + TOK])
    input_grad = joined(finished[:TOK], arrived, core, 1)
    return input_grad, w_grad[:, :128][None], w_grad[:, 128:][None], down_grad[None]


def solution(mesh):
    rows, deep, wide = P(ALL, None), P("node", None, "blk"), P("node", "blk", None)
    return jax.shard_map(
        on_device,
        mesh=mesh,
        in_specs=(rows, rows, rows, rows, deep, deep, wide),
        out_specs=(rows, deep, deep, wide),
        check_vma=False,
    )
```

```python
import jax
import jax.numpy as jnp
import numpy as np
from jax import lax
from jax.experimental import pallas as pl
from jax.experimental.pallas import tpu as pltpu
from jax.sharding import PartitionSpec as P

ALL = ("node", "blk")
SIZES = (4, 2, 4, 4)
AXIS = {"x": 0, "z": 2, "y": 3}
ORDERS = (("x", "y", "z"), ("y", "z", "x"), ("z", "x", "y"))
PARTS = ((0, 9), (9, 18), (18, 28))
TOK = 14
HALF = 3584
WIDE = HALF + 128
UNIT = 24
TILE = 1792
GRAD_TILE = 896
ROWS = 448
BOUNDS = tuple((16 * lo, 16 * hi) for lo, hi in PARTS)
FIRST, SECOND = (1, 3), (3, 1)
OWNERS = ((0, 1, 3, 2), (0, 3, 1, 2))


def swap(value):
    return lax.ppermute(value, ALL, PAIRS["core"])


def hops(values, axes, turn):
    return [lax.ppermute(v, ALL, PAIRS[axis, turn]) for v, axis in zip(values, axes)]


def stage(*values):
    return lax.optimization_barrier(values)


def added(*terms):
    total = terms[0].astype(jnp.float32)
    for term in terms[1:]:
        total = total + term.astype(jnp.float32)
    return total.astype(jnp.bfloat16)


def paired(target):
    pairs = []
    for at in np.ndindex(*SIZES):
        pairs.append((int(np.ravel_multi_index(at, SIZES)), int(np.ravel_multi_index(target(at), SIZES))))
    return pairs


def neighbour(axis, by_core):
    def target(at):
        to = list(at)
        to[axis] = to[axis] ^ by_core[at[1]]
        return tuple(to)

    return target


PAIRS = {"core": paired(lambda at: (at[0], 1 - at[1], at[2], at[3]))}
for _name, _axis in AXIS.items():
    PAIRS[_name, 0] = paired(neighbour(_axis, FIRST))
    PAIRS[_name, 1] = paired(neighbour(_axis, SECOND))


def place(core, pick):
    tables = []
    for c in (0, 1):
        rows, width = pick(c)
        table = np.zeros((len(rows), width), np.float32)
        for r, column in enumerate(rows):
            if column >= 0:
                table[r, column] = 1
        tables.append(table)
    return jnp.where(core == 0, jnp.asarray(tables[0], jnp.bfloat16), jnp.asarray(tables[1], jnp.bfloat16))


def move(table, value):
    return jnp.dot(table, value, preferred_element_type=jnp.float32).astype(jnp.bfloat16)


def pick_first(c):
    rows = []
    for lo, hi in PARTS:
        part = []
        for kind in (0, 1):
            for i in range(lo, hi):
                source = 0 if i // TOK == c else 2 * TOK
                part.append(source + kind * TOK + i % TOK)
        rows += part + [-1] * (UNIT - len(part))
    return rows, 4 * TOK


def pick_joined(n, stride, total):
    def pick(c):
        rows = []
        for kind in (0, 1):
            for j in range(4):
                rows += [OWNERS[c].index(j) * stride + kind * n + i for i in range(n)]
        return rows + [-1] * (total - len(rows)), 4 * stride

    return pick


def pick_split(n, held, padded, blocks):
    def pick(c):
        rows = []
        for q in blocks:
            rows += [OWNERS[c][q] * n + i for i in range(n)] + [-1] * (padded - n)
        return rows, held

    return pick


def pick_last(c):
    rows = []
    for core in (c, 1 - c):
        for t in range(TOK):
            i = core * TOK + t
            p = [p for p in range(3) if PARTS[p][0] <= i < PARTS[p][1]][0]
            rows.append(16 * p + i - PARTS[p][0])
        rows += [-1, -1]
    return rows, 48


def half(value, which, axis):
    size = value.shape[axis] // 2
    return lax.dynamic_slice_in_dim(value, which * size, size, axis)


def joined(own, other, core, axis):
    return jnp.where(core == 0, jnp.concatenate([own, other], axis), jnp.concatenate([other, own], axis))


def dot(a, b, over):
    return lax.dot_general(a, b, (over, ((), ())), preferred_element_type=jnp.float32)


COST = pl.CostEstimate(flops=1, bytes_accessed=1, transcendentals=0)
ACROSS = ((1,), (1,))
ALONG = ((1,), (0,))
DOWN = ((0,), (0,))


def params(grant=60):
    return pltpu.CompilerParams(dimension_semantics=("arbitrary",), vmem_limit_bytes=grant * 1024 * 1024)


def x_rows(blocks):
    return jnp.concatenate([b[: hi - lo, :] for b, (lo, hi) in zip(blocks, BOUNDS)], 0)


def g_rows(blocks):
    return jnp.concatenate([b[hi - lo :, :] for b, (lo, hi) in zip(blocks, BOUNDS)], 0)


def forward_kernel(b0, b1, b2, w_own, w_other, d_own, d_other, sums, sent):
    pre = dot(x_rows((b0, b1, b2)), jnp.concatenate([w_own[...], w_other[...]], 1), ALONG)
    act = dot(g_rows((b0, b1, b2)), jnp.concatenate([d_own[...], d_other[...]], 0), ACROSS)

    @pl.when(pl.program_id(0) == 0)
    def _():
        sums[:, :512] = pre
        sums[:, 512:] = act

    @pl.when(pl.program_id(0) > 0)
    def _():
        sums[:, :512] += pre
        sums[:, 512:] += act
        sent[...] = sums[...].astype(jnp.bfloat16)


def forward(blocks, weights):
    tall = pl.BlockSpec((TILE, 256), lambda i: (i, 0))
    flat = pl.BlockSpec((128, TILE), lambda i: (0, i))
    return pl.pallas_call(
        forward_kernel,
        grid=(HALF // TILE,),
        in_specs=[pl.BlockSpec((b.shape[0], TILE), lambda i: (0, i)) for b in blocks] + [tall, tall, flat, flat],
        out_specs=[pl.BlockSpec((ROWS, 768), lambda i: (0, 0))] * 2,
        out_shape=[jax.ShapeDtypeStruct((ROWS, 768), t) for t in (jnp.float32, jnp.bfloat16)],
        compiler_params=params(),
        cost_estimate=COST,
    )(*blocks, *weights)


def backward_kernel(mine, arrived, t0, t1, t2, chosen, w_own, w_other, delta, activation, p0, p1, p2, held):
    @pl.when(pl.program_id(0) == 0)
    def _():
        for tail, (lo, hi) in zip((t0, t1, t2), BOUNDS):
            gates = dot(tail[hi - lo :, :], chosen[...], ALONG)
            for e in (0, 1):
                near, far = 256 * e, 256 * (1 - e)
                gate = gates[:, e : e + 1]
                pre_gate = mine[lo:hi, near : near + 128] + arrived[lo:hi, far : far + 128]
                pre_up = mine[lo:hi, near + 128 : near + 256] + arrived[lo:hi, far + 128 : far + 256]
                near, far = 512 + 128 * e, 640 - 128 * e
                act_grad = gate * (mine[lo:hi, near : near + 128] + arrived[lo:hi, far : far + 128])
                sigmoid_gate = jax.nn.sigmoid(pre_gate)
                silu_gate = pre_gate * sigmoid_gate
                gate_delta = act_grad * pre_up * sigmoid_gate * (1.0 + pre_gate * (1.0 - sigmoid_gate))
                held[lo:hi, 256 * e : 256 * e + 128] = gate_delta.astype(jnp.bfloat16)
                held[lo:hi, 256 * e + 128 : 256 * e + 256] = (act_grad * silu_gate).astype(jnp.bfloat16)
                activation[lo:hi, 128 * e : 128 * e + 128] = (gate * (silu_gate * pre_up)).astype(jnp.bfloat16)
        delta[...] = held[...]

    total = dot(held[...], jnp.concatenate([w_own[...], w_other[...]], 1), ACROSS).astype(jnp.bfloat16)
    for piece, (lo, hi) in zip((p0, p1, p2), BOUNDS):
        piece[...] = total[lo:hi]


def backward(mine, arrived, blocks, chosen, weights):
    whole = pl.BlockSpec((ROWS, 768), lambda i: (0, 0))
    tall = pl.BlockSpec((TILE, 256), lambda i: (i, 0))
    sizes = [hi - lo for lo, hi in BOUNDS]
    return pl.pallas_call(
        backward_kernel,
        grid=(HALF // TILE,),
        in_specs=[whole, whole]
        + [pl.BlockSpec((b.shape[0], 128), lambda i: (0, HALF // 128)) for b in blocks]
        + [pl.BlockSpec((128, 128), lambda i: (0, 0)), tall, tall],
        out_specs=[pl.BlockSpec((ROWS, 512), lambda i: (0, 0)), pl.BlockSpec((ROWS, 256), lambda i: (0, 0))]
        + [pl.BlockSpec((n, TILE), lambda i: (0, i)) for n in sizes],
        out_shape=[jax.ShapeDtypeStruct((ROWS, 512), jnp.bfloat16), jax.ShapeDtypeStruct((ROWS, 256), jnp.bfloat16)]
        + [jax.ShapeDtypeStruct((n, HALF), jnp.bfloat16) for n in sizes],
        scratch_shapes=[pltpu.VMEM((ROWS, 512), jnp.bfloat16)],
        compiler_params=params(),
        cost_estimate=COST,
    )(mine, arrived, *blocks, chosen, *weights[:2])


def rows_of(refs):
    return jnp.concatenate([r[...] for r in refs], 0)


def tall_kernel(*refs):
    blocks, deltas, (own, other) = refs[:12], refs[12:16], refs[16:]
    total = dot(rows_of(blocks), rows_of(deltas), DOWN)
    own[...] = total[:, :256].astype(jnp.bfloat16)
    other[...] = total[:, 256:].astype(jnp.bfloat16)


def flat_kernel(*refs):
    blocks, activations, (own, other) = refs[:12], refs[12:16], refs[16:]
    total = dot(rows_of(activations), rows_of(blocks), DOWN)
    own[...] = total[:128].astype(jnp.bfloat16)
    other[...] = total[128:].astype(jnp.bfloat16)


def weight_grads(kernel, blocks, hidden, kind, shape, block, index):
    parts = [b for four in blocks for b in four]
    width = hidden[0].shape[1]
    return pl.pallas_call(
        kernel,
        grid=(HALF // GRAD_TILE,),
        in_specs=[pl.BlockSpec((b.shape[0] // 2, GRAD_TILE), lambda i: (kind, i)) for b in parts]
        + [pl.BlockSpec((ROWS, width), lambda i: (0, 0)) for _ in hidden],
        out_specs=[pl.BlockSpec(block, index)] * 2,
        out_shape=[jax.ShapeDtypeStruct(shape, jnp.bfloat16)] * 2,
        compiler_params=params(40),
        cost_estimate=COST,
    )(*parts, *hidden)


def tall_grads(blocks, deltas):
    return weight_grads(tall_kernel, blocks, deltas, 0, (HALF, 256), (GRAD_TILE, 256), lambda i: (i, 0))


def flat_grads(blocks, activations):
    return weight_grads(flat_kernel, blocks, activations, 1, (128, HALF), (128, GRAD_TILE), lambda i: (0, i))


def on_device(tokens, out_grad, expert_ids, gates, w_gate, w_up, w_down):
    node = lax.axis_index("node")
    core = node % 2
    sizes = [hi - lo for lo, hi in PARTS]
    small, middle, large = ([o[i] for o in ORDERS] for i in range(3))

    experts = jnp.arange(WIDE - HALF, dtype=jnp.int32)[None, :]
    gate_sum = jnp.zeros((TOK, WIDE - HALF), jnp.float32)
    for k in range(4):
        gate_sum = gate_sum + jnp.where(expert_ids[:, k : k + 1] == experts, gates[:, k : k + 1].astype(jnp.float32), 0.0)
    gate_sum = jnp.concatenate([jnp.zeros_like(gate_sum), gate_sum], 0).astype(jnp.bfloat16)
    both = jnp.concatenate([tokens, out_grad], 0)
    other = swap(jnp.concatenate([half(both, 1 - core, 1), gate_sum], 1))
    rows = jnp.concatenate([jnp.concatenate([half(both, core, 1), gate_sum], 1), other], 0)
    units = move(place(core, pick_first), rows)
    units = [units[p * UNIT : (p + 1) * UNIT] for p in range(3)]

    def gathered(units, axes, beside):
        first = hops(units, axes, 0)
        if beside:
            first[0], beside = stage(first[0], beside)
        pairs = [jnp.concatenate([u, f], 0) for u, f in zip(units, first)]
        return pairs, hops(pairs, axes, 1), beside

    pairs, others, _ = gathered(units, small, ())
    units = [
        move(place(core, pick_joined(n, UNIT, 80)), jnp.concatenate([p, s], 0))
        for n, p, s in zip(sizes, pairs, others)
    ]
    units[2], raw = stage(units[2], (w_gate[0], w_up[0], w_down[0]))
    w_own = jnp.concatenate([half(raw[0], core, 0), half(raw[1], core, 0)], 1)
    w_other = jnp.concatenate([half(raw[0], 1 - core, 0), half(raw[1], 1 - core, 0)], 1)
    d_own, d_other = half(raw[2], core, 1), half(raw[2], 1 - core, 1)
    pairs, others, (w_own, w_other, d_own, d_other) = gathered(units, middle, [w_own, w_other, d_own, d_other])
    w_other, d_other = swap(w_other), swap(d_other)
    units = [
        move(place(core, pick_joined(4 * n, 80, 32 * n)), jnp.concatenate([p, s], 0))
        for n, p, s in zip(sizes, pairs, others)
    ]
    weights = (w_own, w_other, d_own, d_other)

    wanted = jnp.stack([node, node + 1 - 2 * core])
    chosen = jnp.arange(128)[None, :] == jnp.array([0, 1])[:, None]
    chosen = jnp.sum(
        (jnp.arange(128)[:, None, None] == wanted[None, :, None]) & chosen[None], axis=1
    ).astype(jnp.bfloat16)

    def paced(values, behind):
        pairs = [stage(v, b) for v, b in zip(values, behind)]
        return [p[0] for p in pairs], [p[1] for p in pairs]

    own, sums, done = units, [None] * 4, [None] * 4
    first = hops(own, large, 0)
    sums[0] = forward(own, weights)
    done[0] = backward(sums[0][0], swap(sums[0][1]), own, chosen, weights)
    own, done[0] = stage(own, done[0])
    own, first = paced(own, first)

    second, sums[1] = hops(own, large, 1), forward(first, weights)
    arrived = swap(sums[1][1])
    first, sums[1], arrived = stage(first, sums[1], arrived)
    first, second = paced(first, second)

    far, sums[2] = hops(first, large, 1), forward(second, weights)
    done[2] = backward(sums[2][0], arrived, second, chosen, weights)
    done[1] = backward(sums[1][0], swap(sums[2][1]), first, chosen, weights)
    done[2], done[1] = stage(done[2], done[1])
    pieces, far = paced(done[2][2:], far)

    from_second, sums[3] = hops(pieces, large, 1), forward(far, weights)
    done[3] = backward(sums[3][0], swap(sums[3][1]), far, chosen, weights)
    from_second, done[3] = stage(from_second, done[3])

    every = [own, first, second, far]
    from_far, d_grad = stage(hops(done[3][2:], large, 1), flat_grads(every, [d[1] for d in done]))
    totals = [added(t, f) for t, f in zip(done[1][2:], from_far)]
    from_first, w_grad, d_arrived = stage(hops(totals, large, 0), tall_grads(every, [d[0] for d in done]), swap(d_grad[1]))
    totals = [added(t, s, f) for t, s, f in zip(done[0][2:], from_second, from_first)]

    def reduced(totals, axes, blocks, held, padded, beside):
        outer = [move(place(core, pick_split(n, h, padded, (2, 3))), t) for n, h, t in zip(blocks, held, totals)]
        far = hops(outer, axes, 1)
        inner = [move(place(core, pick_split(n, h, padded, (0, 1))), t) for n, h, t in zip(blocks, held, totals)]
        middle = [added(t[padded:], f[padded:]) for t, f in zip(inner, far)]
        first, beside = stage(hops(middle, axes, 0), beside)
        return [added(t[:padded], f[:padded], g) for t, f, g in zip(inner, far, first)], beside

    totals, w_arrived = reduced(
        totals, middle, [4 * n for n in sizes], [16 * n for n in sizes], 40, swap(w_grad[1])
    )
    w_grad = joined(w_grad[0], w_arrived, core, 0)
    down_grad = joined(d_grad[0], d_arrived, core, 1)
    totals, (w_grad, down_grad) = reduced(totals, small, sizes, [40] * 3, 16, (w_grad, down_grad))
    finished = move(place(core, pick_last), jnp.concatenate(totals, 0))
    arrived = swap(finished[16 : 16 + TOK])
    input_grad = joined(finished[:TOK], arrived, core, 1)
    return input_grad, w_grad[:, :128][None], w_grad[:, 128:][None], down_grad[None]


def solution(mesh):
    rows, deep, wide = P(ALL, None), P("node", None, "blk"), P("node", "blk", None)
    return jax.shard_map(
        on_device,
        mesh=mesh,
        in_specs=(rows, rows, rows, rows, deep, deep, wide),
        out_specs=(rows, deep, deep, wide),
        check_vma=False,
    )
```

```python
import jax
import jax.numpy as jnp
import numpy as np
from jax import lax
from jax.experimental import pallas as pl
from jax.experimental.pallas import tpu as pltpu
from jax.sharding import PartitionSpec as P

ALL = ("node", "blk")
SIZES = (4, 2, 4, 4)
AXIS = {"x": 0, "z": 2, "y": 3}
ORDERS = (("x", "y", "z"), ("y", "z", "x"), ("z", "x", "y"))
PARTS = ((0, 9), (9, 18), (18, 28))
TOK = 14
HALF = 3584
WIDE = HALF + 128
UNIT = 24
TILE = 1792
GRAD_TILE = 896
ROWS = 448
BOUNDS = tuple((16 * lo, 16 * hi) for lo, hi in PARTS)
FIRST, SECOND = (1, 3), (3, 1)
OWNERS = ((0, 1, 3, 2), (0, 3, 1, 2))


def swap(value):
    return lax.ppermute(value, ALL, PAIRS["core"])


def hops(values, axes, turn):
    return [lax.ppermute(v, ALL, PAIRS[axis, turn]) for v, axis in zip(values, axes)]


def stage(*values):
    return lax.optimization_barrier(values)


def added(*terms):
    total = terms[0].astype(jnp.float32)
    for term in terms[1:]:
        total = total + term.astype(jnp.float32)
    return total.astype(jnp.bfloat16)


def paired(target):
    pairs = []
    for at in np.ndindex(*SIZES):
        pairs.append((int(np.ravel_multi_index(at, SIZES)), int(np.ravel_multi_index(target(at), SIZES))))
    return pairs


def neighbour(axis, by_core):
    def target(at):
        to = list(at)
        to[axis] = to[axis] ^ by_core[at[1]]
        return tuple(to)

    return target


PAIRS = {"core": paired(lambda at: (at[0], 1 - at[1], at[2], at[3]))}
for _name, _axis in AXIS.items():
    PAIRS[_name, 0] = paired(neighbour(_axis, FIRST))
    PAIRS[_name, 1] = paired(neighbour(_axis, SECOND))


def place(core, pick):
    tables = []
    for c in (0, 1):
        rows, width = pick(c)
        table = np.zeros((len(rows), width), np.float32)
        for r, column in enumerate(rows):
            if column >= 0:
                table[r, column] = 1
        tables.append(table)
    return jnp.where(core == 0, jnp.asarray(tables[0], jnp.bfloat16), jnp.asarray(tables[1], jnp.bfloat16))


def move(table, value):
    return jnp.dot(table, value, preferred_element_type=jnp.float32).astype(jnp.bfloat16)


def pick_first(c):
    rows = []
    for lo, hi in PARTS:
        part = []
        for kind in (0, 1):
            for i in range(lo, hi):
                source = 0 if i // TOK == c else 2 * TOK
                part.append(source + kind * TOK + i % TOK)
        rows += part + [-1] * (UNIT - len(part))
    return rows, 4 * TOK


def pick_joined(n, stride, total):
    def pick(c):
        rows = []
        for kind in (0, 1):
            for j in range(4):
                rows += [OWNERS[c].index(j) * stride + kind * n + i for i in range(n)]
        return rows + [-1] * (total - len(rows)), 4 * stride

    return pick


def pick_split(n, held, padded, blocks):
    def pick(c):
        rows = []
        for q in blocks:
            rows += [OWNERS[c][q] * n + i for i in range(n)] + [-1] * (padded - n)
        return rows, held

    return pick


def pick_last(c):
    rows = []
    for core in (c, 1 - c):
        for t in range(TOK):
            i = core * TOK + t
            p = [p for p in range(3) if PARTS[p][0] <= i < PARTS[p][1]][0]
            rows.append(16 * p + i - PARTS[p][0])
        rows += [-1, -1]
    return rows, 48


def half(value, which, axis):
    size = value.shape[axis] // 2
    return lax.dynamic_slice_in_dim(value, which * size, size, axis)


def joined(own, other, core, axis):
    return jnp.where(core == 0, jnp.concatenate([own, other], axis), jnp.concatenate([other, own], axis))


def dot(a, b, over):
    return lax.dot_general(a, b, (over, ((), ())), preferred_element_type=jnp.float32)


COST = pl.CostEstimate(flops=1, bytes_accessed=1, transcendentals=0)
ACROSS = ((1,), (1,))
ALONG = ((1,), (0,))
DOWN = ((0,), (0,))


def params(grant=60):
    return pltpu.CompilerParams(dimension_semantics=("arbitrary",), vmem_limit_bytes=grant * 1024 * 1024)


def x_rows(blocks):
    return jnp.concatenate([b[: hi - lo, :] for b, (lo, hi) in zip(blocks, BOUNDS)], 0)


def g_rows(blocks):
    return jnp.concatenate([b[hi - lo :, :] for b, (lo, hi) in zip(blocks, BOUNDS)], 0)


def forward_kernel(b0, b1, b2, w_own, w_other, d_own, d_other, sums, sent):
    pre = dot(x_rows((b0, b1, b2)), jnp.concatenate([w_own[...], w_other[...]], 1), ALONG)
    act = dot(g_rows((b0, b1, b2)), jnp.concatenate([d_own[...], d_other[...]], 0), ACROSS)

    @pl.when(pl.program_id(0) == 0)
    def _():
        sums[:, :512] = pre
        sums[:, 512:] = act

    @pl.when(pl.program_id(0) > 0)
    def _():
        sums[:, :512] += pre
        sums[:, 512:] += act
        sent[...] = sums[...].astype(jnp.bfloat16)


def forward(blocks, weights):
    tall = pl.BlockSpec((TILE, 256), lambda i: (i, 0))
    flat = pl.BlockSpec((128, TILE), lambda i: (0, i))
    return pl.pallas_call(
        forward_kernel,
        grid=(HALF // TILE,),
        in_specs=[pl.BlockSpec((b.shape[0], TILE), lambda i: (0, i)) for b in blocks] + [tall, tall, flat, flat],
        out_specs=[pl.BlockSpec((ROWS, 768), lambda i: (0, 0))] * 2,
        out_shape=[jax.ShapeDtypeStruct((ROWS, 768), t) for t in (jnp.float32, jnp.bfloat16)],
        compiler_params=params(),
        cost_estimate=COST,
    )(*blocks, *weights)


def backward_kernel(mine, arrived, t0, t1, t2, chosen, w_own, w_other, delta, activation, p0, p1, p2, held):
    @pl.when(pl.program_id(0) == 0)
    def _():
        for tail, (lo, hi) in zip((t0, t1, t2), BOUNDS):
            gates = dot(tail[hi - lo :, :], chosen[...], ALONG)
            for e in (0, 1):
                near, far = 256 * e, 256 * (1 - e)
                gate = gates[:, e : e + 1]
                pre_gate = mine[lo:hi, near : near + 128] + arrived[lo:hi, far : far + 128]
                pre_up = mine[lo:hi, near + 128 : near + 256] + arrived[lo:hi, far + 128 : far + 256]
                near, far = 512 + 128 * e, 640 - 128 * e
                act_grad = gate * (mine[lo:hi, near : near + 128] + arrived[lo:hi, far : far + 128])
                sigmoid_gate = jax.nn.sigmoid(pre_gate)
                silu_gate = pre_gate * sigmoid_gate
                gate_delta = act_grad * pre_up * sigmoid_gate * (1.0 + pre_gate * (1.0 - sigmoid_gate))
                held[lo:hi, 256 * e : 256 * e + 128] = gate_delta.astype(jnp.bfloat16)
                held[lo:hi, 256 * e + 128 : 256 * e + 256] = (act_grad * silu_gate).astype(jnp.bfloat16)
                activation[lo:hi, 128 * e : 128 * e + 128] = (gate * (silu_gate * pre_up)).astype(jnp.bfloat16)
        delta[...] = held[...]

    total = dot(held[...], jnp.concatenate([w_own[...], w_other[...]], 1), ACROSS).astype(jnp.bfloat16)
    for piece, (lo, hi) in zip((p0, p1, p2), BOUNDS):
        piece[...] = total[lo:hi]


def backward(mine, arrived, blocks, chosen, weights):
    whole = pl.BlockSpec((ROWS, 768), lambda i: (0, 0))
    tall = pl.BlockSpec((TILE, 256), lambda i: (i, 0))
    sizes = [hi - lo for lo, hi in BOUNDS]
    return pl.pallas_call(
        backward_kernel,
        grid=(HALF // TILE,),
        in_specs=[whole, whole]
        + [pl.BlockSpec((b.shape[0], 128), lambda i: (0, HALF // 128)) for b in blocks]
        + [pl.BlockSpec((128, 128), lambda i: (0, 0)), tall, tall],
        out_specs=[pl.BlockSpec((ROWS, 512), lambda i: (0, 0)), pl.BlockSpec((ROWS, 256), lambda i: (0, 0))]
        + [pl.BlockSpec((n, TILE), lambda i: (0, i)) for n in sizes],
        out_shape=[jax.ShapeDtypeStruct((ROWS, 512), jnp.bfloat16), jax.ShapeDtypeStruct((ROWS, 256), jnp.bfloat16)]
        + [jax.ShapeDtypeStruct((n, HALF), jnp.bfloat16) for n in sizes],
        scratch_shapes=[pltpu.VMEM((ROWS, 512), jnp.bfloat16)],
        compiler_params=params(),
        cost_estimate=COST,
    )(mine, arrived, *blocks, chosen, *weights[:2])


def rows_of(refs):
    return jnp.concatenate([r[...] for r in refs], 0)


def tall_kernel(*refs):
    blocks, deltas, (own, other) = refs[:12], refs[12:16], refs[16:]
    total = dot(rows_of(blocks), rows_of(deltas), DOWN)
    own[...] = total[:, :256].astype(jnp.bfloat16)
    other[...] = total[:, 256:].astype(jnp.bfloat16)


def flat_kernel(*refs):
    blocks, activations, (own, other) = refs[:12], refs[12:16], refs[16:]
    total = dot(rows_of(activations), rows_of(blocks), DOWN)
    own[...] = total[:128].astype(jnp.bfloat16)
    other[...] = total[128:].astype(jnp.bfloat16)


def weight_grads(kernel, blocks, hidden, kind, shape, block, index):
    parts = [b for four in blocks for b in four]
    width = hidden[0].shape[1]
    return pl.pallas_call(
        kernel,
        grid=(HALF // GRAD_TILE,),
        in_specs=[pl.BlockSpec((b.shape[0] // 2, GRAD_TILE), lambda i: (kind, i)) for b in parts]
        + [pl.BlockSpec((ROWS, width), lambda i: (0, 0)) for _ in hidden],
        out_specs=[pl.BlockSpec(block, index)] * 2,
        out_shape=[jax.ShapeDtypeStruct(shape, jnp.bfloat16)] * 2,
        compiler_params=params(40),
        cost_estimate=COST,
    )(*parts, *hidden)


def tall_grads(blocks, deltas):
    return weight_grads(tall_kernel, blocks, deltas, 0, (HALF, 256), (GRAD_TILE, 256), lambda i: (i, 0))


def flat_grads(blocks, activations):
    return weight_grads(flat_kernel, blocks, activations, 1, (128, HALF), (128, GRAD_TILE), lambda i: (0, i))


def on_device(tokens, out_grad, expert_ids, gates, w_gate, w_up, w_down):
    node = lax.axis_index("node")
    core = node % 2
    sizes = [hi - lo for lo, hi in PARTS]
    small, middle, large = ([o[i] for o in ORDERS] for i in range(3))

    experts = jnp.arange(WIDE - HALF, dtype=jnp.int32)[None, :]
    gate_sum = jnp.zeros((TOK, WIDE - HALF), jnp.float32)
    for k in range(4):
        gate_sum = gate_sum + jnp.where(expert_ids[:, k : k + 1] == experts, gates[:, k : k + 1].astype(jnp.float32), 0.0)
    gate_sum = jnp.concatenate([jnp.zeros_like(gate_sum), gate_sum], 0).astype(jnp.bfloat16)
    both = jnp.concatenate([tokens, out_grad], 0)
    other = swap(jnp.concatenate([half(both, 1 - core, 1), gate_sum], 1))
    rows = jnp.concatenate([jnp.concatenate([half(both, core, 1), gate_sum], 1), other], 0)
    units = move(place(core, pick_first), rows)
    units = [units[p * UNIT : (p + 1) * UNIT] for p in range(3)]

    def gathered(units, axes, beside):
        first = hops(units, axes, 0)
        if beside:
            first[0], beside = stage(first[0], beside)
        pairs = [jnp.concatenate([u, f], 0) for u, f in zip(units, first)]
        return pairs, hops(pairs, axes, 1), beside

    pairs, others, _ = gathered(units, small, ())
    units = [
        move(place(core, pick_joined(n, UNIT, 80)), jnp.concatenate([p, s], 0))
        for n, p, s in zip(sizes, pairs, others)
    ]
    units[2], raw = stage(units[2], (w_gate[0], w_up[0], w_down[0]))
    w_own = jnp.concatenate([half(raw[0], core, 0), half(raw[1], core, 0)], 1)
    w_other = jnp.concatenate([half(raw[0], 1 - core, 0), half(raw[1], 1 - core, 0)], 1)
    d_own, d_other = half(raw[2], core, 1), half(raw[2], 1 - core, 1)
    pairs, others, (w_own, w_other, d_own, d_other) = gathered(units, middle, [w_own, w_other, d_own, d_other])
    w_other, d_other = swap(w_other), swap(d_other)
    tables = [place(core, pick_joined(4 * n, 80, 32 * n)) for n in sizes]
    placed = [move(t[:, :160], p) for t, p in zip(tables, pairs)]
    ready = [stage(s, p, t[:, 160:]) for s, p, t in zip(others, placed, tables)]
    units = [
        (jnp.dot(t, s, preferred_element_type=jnp.float32) + p.astype(jnp.float32)).astype(jnp.bfloat16)
        for s, p, t in ready
    ]
    weights = (w_own, w_other, d_own, d_other)

    wanted = jnp.stack([node, node + 1 - 2 * core])
    chosen = jnp.arange(128)[None, :] == jnp.array([0, 1])[:, None]
    chosen = jnp.sum(
        (jnp.arange(128)[:, None, None] == wanted[None, :, None]) & chosen[None], axis=1
    ).astype(jnp.bfloat16)

    def paced(values, behind):
        pairs = [stage(v, b) for v, b in zip(values, behind)]
        return [p[0] for p in pairs], [p[1] for p in pairs]

    own, sums, done = units, [None] * 4, [None] * 4
    first = hops(own, large, 0)
    sums[0] = forward(own, weights)
    done[0] = backward(sums[0][0], swap(sums[0][1]), own, chosen, weights)
    own, done[0] = stage(own, done[0])
    own, first = paced(own, first)

    second, sums[1] = hops(own, large, 1), forward(first, weights)
    arrived = swap(sums[1][1])
    first, sums[1], arrived = stage(first, sums[1], arrived)
    first, second = paced(first, second)

    far, sums[2] = hops(first, large, 1), forward(second, weights)
    done[2] = backward(sums[2][0], arrived, second, chosen, weights)
    done[1] = backward(sums[1][0], swap(sums[2][1]), first, chosen, weights)
    done[2], done[1] = stage(done[2], done[1])
    pieces, far = paced(done[2][2:], far)

    from_second, sums[3] = hops(pieces, large, 1), forward(far, weights)
    done[3] = backward(sums[3][0], swap(sums[3][1]), far, chosen, weights)
    from_second, done[3] = stage(from_second, done[3])

    every = [own, first, second, far]
    from_far, d_grad = stage(hops(done[3][2:], large, 1), flat_grads(every, [d[1] for d in done]))
    totals = [added(t, f) for t, f in zip(done[1][2:], from_far)]
    from_first, w_grad, d_arrived = stage(hops(totals, large, 0), tall_grads(every, [d[0] for d in done]), swap(d_grad[1]))
    totals = [added(t, s, f) for t, s, f in zip(done[0][2:], from_second, from_first)]

    def reduced(totals, axes, blocks, held, padded, beside):
        outer = [move(place(core, pick_split(n, h, padded, (2, 3))), t) for n, h, t in zip(blocks, held, totals)]
        far = hops(outer, axes, 1)
        inner = [move(place(core, pick_split(n, h, padded, (0, 1))), t) for n, h, t in zip(blocks, held, totals)]
        middle = [added(t[padded:], f[padded:]) for t, f in zip(inner, far)]
        first, beside = stage(hops(middle, axes, 0), beside)
        return [added(t[:padded], f[:padded], g) for t, f, g in zip(inner, far, first)], beside

    totals, w_arrived = reduced(
        totals, middle, [4 * n for n in sizes], [16 * n for n in sizes], 40, swap(w_grad[1])
    )
    w_grad = joined(w_grad[0], w_arrived, core, 0)
    down_grad = joined(d_grad[0], d_arrived, core, 1)
    totals, (w_grad, down_grad) = reduced(totals, small, sizes, [40] * 3, 16, (w_grad, down_grad))
    finished = move(place(core, pick_last), jnp.concatenate(totals, 0))
    arrived = swap(finished[16 : 16 + TOK])
    input_grad = joined(finished[:TOK], arrived, core, 1)
    return input_grad, w_grad[:, :128][None], w_grad[:, 128:][None], down_grad[None]


def solution(mesh):
    rows, deep, wide = P(ALL, None), P("node", None, "blk"), P("node", "blk", None)
    return jax.shard_map(
        on_device,
        mesh=mesh,
        in_specs=(rows, rows, rows, rows, deep, deep, wide),
        out_specs=(rows, deep, deep, wide),
        check_vma=False,
    )
```

```python
import jax
import jax.numpy as jnp
import numpy as np
from jax import lax
from jax.experimental import pallas as pl
from jax.experimental.pallas import tpu as pltpu
from jax.sharding import PartitionSpec as P

ALL = ("node", "blk")
SIZES = (4, 2, 4, 4)
AXIS = {"x": 0, "z": 2, "y": 3}
ORDERS = (("x", "y", "z"), ("y", "z", "x"), ("z", "x", "y"))
PARTS = ((0, 9), (9, 18), (18, 28))
TOK = 14
HALF = 3584
WIDE = HALF + 128
UNIT = 24
TILE = 1792
GRAD_TILE = 896
ROWS = 448
BOUNDS = tuple((16 * lo, 16 * hi) for lo, hi in PARTS)
FIRST, SECOND = (1, 3), (3, 1)
OWNERS = ((0, 1, 3, 2), (0, 3, 1, 2))


def swap(value):
    return lax.ppermute(value, ALL, PAIRS["core"])


def hops(values, axes, turn):
    return [lax.ppermute(v, ALL, PAIRS[axis, turn]) for v, axis in zip(values, axes)]


def stage(*values):
    return lax.optimization_barrier(values)


def added(*terms):
    total = terms[0].astype(jnp.float32)
    for term in terms[1:]:
        total = total + term.astype(jnp.float32)
    return total.astype(jnp.bfloat16)


def paired(target):
    pairs = []
    for at in np.ndindex(*SIZES):
        pairs.append((int(np.ravel_multi_index(at, SIZES)), int(np.ravel_multi_index(target(at), SIZES))))
    return pairs


def neighbour(axis, by_core):
    def target(at):
        to = list(at)
        to[axis] = to[axis] ^ by_core[at[1]]
        return tuple(to)

    return target


PAIRS = {"core": paired(lambda at: (at[0], 1 - at[1], at[2], at[3]))}
for _name, _axis in AXIS.items():
    PAIRS[_name, 0] = paired(neighbour(_axis, FIRST))
    PAIRS[_name, 1] = paired(neighbour(_axis, SECOND))


def place(core, pick):
    tables = []
    for c in (0, 1):
        rows, width = pick(c)
        table = np.zeros((len(rows), width), np.float32)
        for r, column in enumerate(rows):
            if column >= 0:
                table[r, column] = 1
        tables.append(table)
    return jnp.where(core == 0, jnp.asarray(tables[0], jnp.bfloat16), jnp.asarray(tables[1], jnp.bfloat16))


def move(table, value):
    return jnp.dot(table, value, preferred_element_type=jnp.float32).astype(jnp.bfloat16)


def pick_first(c):
    rows = []
    for lo, hi in PARTS:
        part = []
        for kind in (0, 1):
            for i in range(lo, hi):
                source = 0 if i // TOK == c else 2 * TOK
                part.append(source + kind * TOK + i % TOK)
        rows += part + [-1] * (UNIT - len(part))
    return rows, 4 * TOK


def pick_joined(n, stride, total):
    def pick(c):
        rows = []
        for kind in (0, 1):
            for j in range(4):
                rows += [OWNERS[c].index(j) * stride + kind * n + i for i in range(n)]
        return rows + [-1] * (total - len(rows)), 4 * stride

    return pick


def pick_split(n, held, padded, blocks):
    def pick(c):
        rows = []
        for q in blocks:
            rows += [OWNERS[c][q] * n + i for i in range(n)] + [-1] * (padded - n)
        return rows, held

    return pick


def pick_last(c):
    rows = []
    for core in (c, 1 - c):
        for t in range(TOK):
            i = core * TOK + t
            p = [p for p in range(3) if PARTS[p][0] <= i < PARTS[p][1]][0]
            rows.append(16 * p + i - PARTS[p][0])
        rows += [-1, -1]
    return rows, 48


def half(value, which, axis):
    size = value.shape[axis] // 2
    return lax.dynamic_slice_in_dim(value, which * size, size, axis)


def joined(own, other, core, axis):
    return jnp.where(core == 0, jnp.concatenate([own, other], axis), jnp.concatenate([other, own], axis))


def dot(a, b, over):
    return lax.dot_general(a, b, (over, ((), ())), preferred_element_type=jnp.float32)


COST = pl.CostEstimate(flops=1, bytes_accessed=1, transcendentals=0)
ACROSS = ((1,), (1,))
ALONG = ((1,), (0,))
DOWN = ((0,), (0,))


def params(grant=60):
    return pltpu.CompilerParams(dimension_semantics=("arbitrary",), vmem_limit_bytes=grant * 1024 * 1024)


def x_rows(blocks):
    return jnp.concatenate([b[: hi - lo, :] for b, (lo, hi) in zip(blocks, BOUNDS)], 0)


def g_rows(blocks):
    return jnp.concatenate([b[hi - lo :, :] for b, (lo, hi) in zip(blocks, BOUNDS)], 0)


def forward_kernel(b0, b1, b2, w_own, w_other, d_own, d_other, sums, sent):
    pre = dot(x_rows((b0, b1, b2)), jnp.concatenate([w_own[...], w_other[...]], 1), ALONG)
    act = dot(g_rows((b0, b1, b2)), jnp.concatenate([d_own[...], d_other[...]], 0), ACROSS)

    @pl.when(pl.program_id(0) == 0)
    def _():
        sums[:, :512] = pre
        sums[:, 512:] = act

    @pl.when(pl.program_id(0) > 0)
    def _():
        sums[:, :512] += pre
        sums[:, 512:] += act
        sent[...] = sums[...].astype(jnp.bfloat16)


def forward(blocks, weights, grant=60):
    tall = pl.BlockSpec((TILE, 256), lambda i: (i, 0))
    flat = pl.BlockSpec((128, TILE), lambda i: (0, i))
    return pl.pallas_call(
        forward_kernel,
        grid=(HALF // TILE,),
        in_specs=[pl.BlockSpec((b.shape[0], TILE), lambda i: (0, i)) for b in blocks] + [tall, tall, flat, flat],
        out_specs=[pl.BlockSpec((ROWS, 768), lambda i: (0, 0))] * 2,
        out_shape=[jax.ShapeDtypeStruct((ROWS, 768), t) for t in (jnp.float32, jnp.bfloat16)],
        compiler_params=params(grant),
        cost_estimate=COST,
    )(*blocks, *weights)


def backward_kernel(mine, arrived, t0, t1, t2, chosen, w_own, w_other, delta, activation, p0, p1, p2, held):
    @pl.when(pl.program_id(0) == 0)
    def _():
        for tail, (lo, hi) in zip((t0, t1, t2), BOUNDS):
            gates = dot(tail[hi - lo :, :], chosen[...], ALONG)
            for e in (0, 1):
                near, far = 256 * e, 256 * (1 - e)
                gate = gates[:, e : e + 1]
                pre_gate = mine[lo:hi, near : near + 128] + arrived[lo:hi, far : far + 128]
                pre_up = mine[lo:hi, near + 128 : near + 256] + arrived[lo:hi, far + 128 : far + 256]
                near, far = 512 + 128 * e, 640 - 128 * e
                act_grad = gate * (mine[lo:hi, near : near + 128] + arrived[lo:hi, far : far + 128])
                sigmoid_gate = jax.nn.sigmoid(pre_gate)
                silu_gate = pre_gate * sigmoid_gate
                gate_delta = act_grad * pre_up * sigmoid_gate * (1.0 + pre_gate * (1.0 - sigmoid_gate))
                held[lo:hi, 256 * e : 256 * e + 128] = gate_delta.astype(jnp.bfloat16)
                held[lo:hi, 256 * e + 128 : 256 * e + 256] = (act_grad * silu_gate).astype(jnp.bfloat16)
                activation[lo:hi, 128 * e : 128 * e + 128] = (gate * (silu_gate * pre_up)).astype(jnp.bfloat16)
        delta[...] = held[...]

    total = dot(held[...], jnp.concatenate([w_own[...], w_other[...]], 1), ACROSS).astype(jnp.bfloat16)
    for piece, (lo, hi) in zip((p0, p1, p2), BOUNDS):
        piece[...] = total[lo:hi]


def backward(mine, arrived, blocks, chosen, weights, grant=60):
    whole = pl.BlockSpec((ROWS, 768), lambda i: (0, 0))
    tall = pl.BlockSpec((TILE, 256), lambda i: (i, 0))
    sizes = [hi - lo for lo, hi in BOUNDS]
    return pl.pallas_call(
        backward_kernel,
        grid=(HALF // TILE,),
        in_specs=[whole, whole]
        + [pl.BlockSpec((b.shape[0], 128), lambda i: (0, HALF // 128)) for b in blocks]
        + [pl.BlockSpec((128, 128), lambda i: (0, 0)), tall, tall],
        out_specs=[pl.BlockSpec((ROWS, 512), lambda i: (0, 0)), pl.BlockSpec((ROWS, 256), lambda i: (0, 0))]
        + [pl.BlockSpec((n, TILE), lambda i: (0, i)) for n in sizes],
        out_shape=[jax.ShapeDtypeStruct((ROWS, 512), jnp.bfloat16), jax.ShapeDtypeStruct((ROWS, 256), jnp.bfloat16)]
        + [jax.ShapeDtypeStruct((n, HALF), jnp.bfloat16) for n in sizes],
        scratch_shapes=[pltpu.VMEM((ROWS, 512), jnp.bfloat16)],
        compiler_params=params(grant),
        cost_estimate=COST,
    )(mine, arrived, *blocks, chosen, *weights[:2])


def rows_of(refs):
    return jnp.concatenate([r[...] for r in refs], 0)


def tall_kernel(*refs):
    blocks, deltas, (own, other) = refs[:12], refs[12:16], refs[16:]
    total = dot(rows_of(blocks), rows_of(deltas), DOWN)
    own[...] = total[:, :256].astype(jnp.bfloat16)
    other[...] = total[:, 256:].astype(jnp.bfloat16)


def flat_kernel(*refs):
    blocks, activations, (own, other) = refs[:12], refs[12:16], refs[16:]
    total = dot(rows_of(activations), rows_of(blocks), DOWN)
    own[...] = total[:128].astype(jnp.bfloat16)
    other[...] = total[128:].astype(jnp.bfloat16)


def weight_grads(kernel, blocks, hidden, kind, shape, block, index):
    parts = [b for four in blocks for b in four]
    width = hidden[0].shape[1]
    return pl.pallas_call(
        kernel,
        grid=(HALF // GRAD_TILE,),
        in_specs=[pl.BlockSpec((b.shape[0] // 2, GRAD_TILE), lambda i: (kind, i)) for b in parts]
        + [pl.BlockSpec((ROWS, width), lambda i: (0, 0)) for _ in hidden],
        out_specs=[pl.BlockSpec(block, index)] * 2,
        out_shape=[jax.ShapeDtypeStruct(shape, jnp.bfloat16)] * 2,
        compiler_params=params(40),
        cost_estimate=COST,
    )(*parts, *hidden)


def tall_grads(blocks, deltas):
    return weight_grads(tall_kernel, blocks, deltas, 0, (HALF, 256), (GRAD_TILE, 256), lambda i: (i, 0))


def flat_grads(blocks, activations):
    return weight_grads(flat_kernel, blocks, activations, 1, (128, HALF), (128, GRAD_TILE), lambda i: (0, i))


def on_device(tokens, out_grad, expert_ids, gates, w_gate, w_up, w_down):
    node = lax.axis_index("node")
    core = node % 2
    sizes = [hi - lo for lo, hi in PARTS]
    small, middle, large = ([o[i] for o in ORDERS] for i in range(3))

    experts = jnp.arange(WIDE - HALF, dtype=jnp.int32)[None, :]
    gate_sum = jnp.zeros((TOK, WIDE - HALF), jnp.float32)
    for k in range(4):
        gate_sum = gate_sum + jnp.where(expert_ids[:, k : k + 1] == experts, gates[:, k : k + 1].astype(jnp.float32), 0.0)
    gate_sum = jnp.concatenate([jnp.zeros_like(gate_sum), gate_sum], 0).astype(jnp.bfloat16)
    both = jnp.concatenate([tokens, out_grad], 0)
    other = swap(jnp.concatenate([half(both, 1 - core, 1), gate_sum], 1))
    rows = jnp.concatenate([jnp.concatenate([half(both, core, 1), gate_sum], 1), other], 0)
    units = move(place(core, pick_first), rows)
    units = [units[p * UNIT : (p + 1) * UNIT] for p in range(3)]

    def gathered(units, axes, beside):
        first = hops(units, axes, 0)
        if beside:
            first[0], beside = stage(first[0], beside)
        pairs = [jnp.concatenate([u, f], 0) for u, f in zip(units, first)]
        return pairs, hops(pairs, axes, 1), beside

    pairs, others, _ = gathered(units, small, ())
    units = [
        move(place(core, pick_joined(n, UNIT, 80)), jnp.concatenate([p, s], 0))
        for n, p, s in zip(sizes, pairs, others)
    ]
    units[2], raw = stage(units[2], (w_gate[0], w_up[0], w_down[0]))
    w_own = jnp.concatenate([half(raw[0], core, 0), half(raw[1], core, 0)], 1)
    w_other = jnp.concatenate([half(raw[0], 1 - core, 0), half(raw[1], 1 - core, 0)], 1)
    d_own, d_other = half(raw[2], core, 1), half(raw[2], 1 - core, 1)
    pairs, others, (w_own, w_other, d_own, d_other) = gathered(units, middle, [w_own, w_other, d_own, d_other])
    w_other, d_other = swap(w_other), swap(d_other)
    units = [
        move(place(core, pick_joined(4 * n, 80, 32 * n)), jnp.concatenate([p, s], 0))
        for n, p, s in zip(sizes, pairs, others)
    ]
    weights = (w_own, w_other, d_own, d_other)

    wanted = jnp.stack([node, node + 1 - 2 * core])
    chosen = jnp.arange(128)[None, :] == jnp.array([0, 1])[:, None]
    chosen = jnp.sum(
        (jnp.arange(128)[:, None, None] == wanted[None, :, None]) & chosen[None], axis=1
    ).astype(jnp.bfloat16)

    def paced(values, behind):
        pairs = [stage(v, b) for v, b in zip(values, behind)]
        return [p[0] for p in pairs], [p[1] for p in pairs]

    own, sums, done = units, [None] * 4, [None] * 4
    first = hops(own, large, 0)
    sums[0] = forward(own, weights)
    done[0] = backward(sums[0][0], swap(sums[0][1]), own, chosen, weights)
    own, done[0] = stage(own, done[0])
    own, first = paced(own, first)

    second, sums[1] = hops(own, large, 1), forward(first, weights)
    arrived = swap(sums[1][1])
    first, sums[1], arrived = stage(first, sums[1], arrived)
    first, second = paced(first, second)

    far, sums[2] = hops(first, large, 1), forward(second, weights)
    done[2] = backward(sums[2][0], arrived, second, chosen, weights)
    done[1] = backward(sums[1][0], swap(sums[2][1]), first, chosen, weights)
    done[2], done[1] = stage(done[2], done[1])
    pieces, far = paced(done[2][2:], far)

    from_second, sums[3] = hops(pieces, large, 1), forward(far, weights, 44)
    done[3] = backward(sums[3][0], swap(sums[3][1]), far, chosen, weights, 44)
    from_second, done[3] = stage(from_second, done[3])

    every = [own, first, second, far]
    from_far, d_grad = stage(hops(done[3][2:], large, 1), flat_grads(every, [d[1] for d in done]))
    totals = [added(t, f) for t, f in zip(done[1][2:], from_far)]
    from_first, w_grad, d_arrived = stage(hops(totals, large, 0), tall_grads(every, [d[0] for d in done]), swap(d_grad[1]))
    totals = [added(t, s, f) for t, s, f in zip(done[0][2:], from_second, from_first)]

    def reduced(totals, axes, blocks, held, padded, beside):
        outer = [move(place(core, pick_split(n, h, padded, (2, 3))), t) for n, h, t in zip(blocks, held, totals)]
        far = hops(outer, axes, 1)
        inner = [move(place(core, pick_split(n, h, padded, (0, 1))), t) for n, h, t in zip(blocks, held, totals)]
        middle = [added(t[padded:], f[padded:]) for t, f in zip(inner, far)]
        first, beside = stage(hops(middle, axes, 0), beside)
        return [added(t[:padded], f[:padded], g) for t, f, g in zip(inner, far, first)], beside

    totals, w_arrived = reduced(
        totals, middle, [4 * n for n in sizes], [16 * n for n in sizes], 40, swap(w_grad[1])
    )
    w_grad = joined(w_grad[0], w_arrived, core, 0)
    down_grad = joined(d_grad[0], d_arrived, core, 1)
    totals, (w_grad, down_grad) = reduced(totals, small, sizes, [40] * 3, 16, (w_grad, down_grad))
    finished = move(place(core, pick_last), jnp.concatenate(totals, 0))
    arrived = swap(finished[16 : 16 + TOK])
    input_grad = joined(finished[:TOK], arrived, core, 1)
    return input_grad, w_grad[:, :128][None], w_grad[:, 128:][None], down_grad[None]


def solution(mesh):
    rows, deep, wide = P(ALL, None), P("node", None, "blk"), P("node", "blk", None)
    return jax.shard_map(
        on_device,
        mesh=mesh,
        in_specs=(rows, rows, rows, rows, deep, deep, wide),
        out_specs=(rows, deep, deep, wide),
        check_vma=False,
    )
```

```python
import jax
import jax.numpy as jnp
import numpy as np
from jax import lax
from jax.experimental import pallas as pl
from jax.experimental.pallas import tpu as pltpu
from jax.sharding import PartitionSpec as P

ALL = ("node", "blk")
SIZES = (4, 2, 4, 4)
AXIS = {"x": 0, "z": 2, "y": 3}
ORDERS = (("x", "y", "z"), ("y", "z", "x"), ("z", "x", "y"))
PARTS = ((0, 9), (9, 18), (18, 28))
TOK = 14
HALF = 3584
WIDE = HALF + 128
UNIT = 24
TILE = 1792
GRAD_TILE = 896
ROWS = 448
BOUNDS = tuple((16 * lo, 16 * hi) for lo, hi in PARTS)
FIRST, SECOND = (1, 3), (3, 1)
OWNERS = ((0, 1, 3, 2), (0, 3, 1, 2))


def swap(value):
    return lax.ppermute(value, ALL, PAIRS["core"])


def hops(values, axes, turn):
    return [lax.ppermute(v, ALL, PAIRS[axis, turn]) for v, axis in zip(values, axes)]


def stage(*values):
    return lax.optimization_barrier(values)


def added(*terms):
    total = terms[0].astype(jnp.float32)
    for term in terms[1:]:
        total = total + term.astype(jnp.float32)
    return total.astype(jnp.bfloat16)


def paired(target):
    pairs = []
    for at in np.ndindex(*SIZES):
        pairs.append((int(np.ravel_multi_index(at, SIZES)), int(np.ravel_multi_index(target(at), SIZES))))
    return pairs


def neighbour(axis, by_core):
    def target(at):
        to = list(at)
        to[axis] = to[axis] ^ by_core[at[1]]
        return tuple(to)

    return target


PAIRS = {"core": paired(lambda at: (at[0], 1 - at[1], at[2], at[3]))}
for _name, _axis in AXIS.items():
    PAIRS[_name, 0] = paired(neighbour(_axis, FIRST))
    PAIRS[_name, 1] = paired(neighbour(_axis, SECOND))


def place(core, pick):
    tables = []
    for c in (0, 1):
        rows, width = pick(c)
        table = np.zeros((len(rows), width), np.float32)
        for r, column in enumerate(rows):
            if column >= 0:
                table[r, column] = 1
        tables.append(table)
    return jnp.where(core == 0, jnp.asarray(tables[0], jnp.bfloat16), jnp.asarray(tables[1], jnp.bfloat16))


def move(table, value):
    return jnp.dot(table, value, preferred_element_type=jnp.float32).astype(jnp.bfloat16)


def pick_first(c):
    rows = []
    for lo, hi in PARTS:
        part = []
        for kind in (0, 1):
            for i in range(lo, hi):
                source = 0 if i // TOK == c else 2 * TOK
                part.append(source + kind * TOK + i % TOK)
        rows += part + [-1] * (UNIT - len(part))
    return rows, 4 * TOK


def pick_joined(n, stride, total):
    def pick(c):
        rows = []
        for kind in (0, 1):
            for j in range(4):
                rows += [OWNERS[c].index(j) * stride + kind * n + i for i in range(n)]
        return rows + [-1] * (total - len(rows)), 4 * stride

    return pick


def pick_split(n, held, padded, blocks):
    def pick(c):
        rows = []
        for q in blocks:
            rows += [OWNERS[c][q] * n + i for i in range(n)] + [-1] * (padded - n)
        return rows, held

    return pick


def pick_last(c):
    rows = []
    for core in (c, 1 - c):
        for t in range(TOK):
            i = core * TOK + t
            p = [p for p in range(3) if PARTS[p][0] <= i < PARTS[p][1]][0]
            rows.append(16 * p + i - PARTS[p][0])
        rows += [-1, -1]
    return rows, 48


def half(value, which, axis):
    size = value.shape[axis] // 2
    return lax.dynamic_slice_in_dim(value, which * size, size, axis)


def joined(own, other, core, axis):
    return jnp.where(core == 0, jnp.concatenate([own, other], axis), jnp.concatenate([other, own], axis))


def dot(a, b, over):
    return lax.dot_general(a, b, (over, ((), ())), preferred_element_type=jnp.float32)


COST = pl.CostEstimate(flops=1, bytes_accessed=1, transcendentals=0)
ACROSS = ((1,), (1,))
ALONG = ((1,), (0,))
DOWN = ((0,), (0,))


def params(grant=60):
    return pltpu.CompilerParams(dimension_semantics=("arbitrary",), vmem_limit_bytes=grant * 1024 * 1024)


def x_rows(blocks):
    return jnp.concatenate([b[: hi - lo, :] for b, (lo, hi) in zip(blocks, BOUNDS)], 0)


def g_rows(blocks):
    return jnp.concatenate([b[hi - lo :, :] for b, (lo, hi) in zip(blocks, BOUNDS)], 0)


def forward_kernel(b0, b1, b2, w_own, w_other, d_own, d_other, sums, sent):
    pre = dot(x_rows((b0, b1, b2)), jnp.concatenate([w_own[...], w_other[...]], 1), ALONG)
    act = dot(g_rows((b0, b1, b2)), jnp.concatenate([d_own[...], d_other[...]], 0), ACROSS)

    @pl.when(pl.program_id(0) == 0)
    def _():
        sums[:, :512] = pre
        sums[:, 512:] = act

    @pl.when(pl.program_id(0) > 0)
    def _():
        sums[:, :512] += pre
        sums[:, 512:] += act
        sent[...] = sums[...].astype(jnp.bfloat16)


def forward(blocks, weights, grant=60):
    tall = pl.BlockSpec((TILE, 256), lambda i: (i, 0))
    flat = pl.BlockSpec((128, TILE), lambda i: (0, i))
    return pl.pallas_call(
        forward_kernel,
        grid=(HALF // TILE,),
        in_specs=[pl.BlockSpec((b.shape[0], TILE), lambda i: (0, i)) for b in blocks] + [tall, tall, flat, flat],
        out_specs=[pl.BlockSpec((ROWS, 768), lambda i: (0, 0))] * 2,
        out_shape=[jax.ShapeDtypeStruct((ROWS, 768), t) for t in (jnp.float32, jnp.bfloat16)],
        compiler_params=params(grant),
        cost_estimate=COST,
    )(*blocks, *weights)


def backward_kernel(mine, arrived, t0, t1, t2, chosen, w_own, w_other, delta, activation, p0, p1, p2, held):
    @pl.when(pl.program_id(0) == 0)
    def _():
        for tail, (lo, hi) in zip((t0, t1, t2), BOUNDS):
            gates = dot(tail[hi - lo :, :], chosen[...], ALONG)
            for e in (0, 1):
                near, far = 256 * e, 256 * (1 - e)
                gate = gates[:, e : e + 1]
                pre_gate = mine[lo:hi, near : near + 128] + arrived[lo:hi, far : far + 128]
                pre_up = mine[lo:hi, near + 128 : near + 256] + arrived[lo:hi, far + 128 : far + 256]
                near, far = 512 + 128 * e, 640 - 128 * e
                act_grad = gate * (mine[lo:hi, near : near + 128] + arrived[lo:hi, far : far + 128])
                sigmoid_gate = jax.nn.sigmoid(pre_gate)
                silu_gate = pre_gate * sigmoid_gate
                gate_delta = act_grad * pre_up * sigmoid_gate * (1.0 + pre_gate * (1.0 - sigmoid_gate))
                held[lo:hi, 256 * e : 256 * e + 128] = gate_delta.astype(jnp.bfloat16)
                held[lo:hi, 256 * e + 128 : 256 * e + 256] = (act_grad * silu_gate).astype(jnp.bfloat16)
                activation[lo:hi, 128 * e : 128 * e + 128] = (gate * (silu_gate * pre_up)).astype(jnp.bfloat16)
        delta[...] = held[...]

    total = dot(held[...], jnp.concatenate([w_own[...], w_other[...]], 1), ACROSS).astype(jnp.bfloat16)
    for piece, (lo, hi) in zip((p0, p1, p2), BOUNDS):
        piece[...] = total[lo:hi]


def backward(mine, arrived, blocks, chosen, weights, grant=60):
    whole = pl.BlockSpec((ROWS, 768), lambda i: (0, 0))
    tall = pl.BlockSpec((TILE, 256), lambda i: (i, 0))
    sizes = [hi - lo for lo, hi in BOUNDS]
    return pl.pallas_call(
        backward_kernel,
        grid=(HALF // TILE,),
        in_specs=[whole, whole]
        + [pl.BlockSpec((b.shape[0], 128), lambda i: (0, HALF // 128)) for b in blocks]
        + [pl.BlockSpec((128, 128), lambda i: (0, 0)), tall, tall],
        out_specs=[pl.BlockSpec((ROWS, 512), lambda i: (0, 0)), pl.BlockSpec((ROWS, 256), lambda i: (0, 0))]
        + [pl.BlockSpec((n, TILE), lambda i: (0, i)) for n in sizes],
        out_shape=[jax.ShapeDtypeStruct((ROWS, 512), jnp.bfloat16), jax.ShapeDtypeStruct((ROWS, 256), jnp.bfloat16)]
        + [jax.ShapeDtypeStruct((n, HALF), jnp.bfloat16) for n in sizes],
        scratch_shapes=[pltpu.VMEM((ROWS, 512), jnp.bfloat16)],
        compiler_params=params(grant),
        cost_estimate=COST,
    )(mine, arrived, *blocks, chosen, *weights[:2])


def rows_of(refs):
    return jnp.concatenate([r[...] for r in refs], 0)


def tall_kernel(*refs):
    blocks, deltas, (own, other) = refs[:12], refs[12:16], refs[16:]
    total = dot(rows_of(blocks), rows_of(deltas), DOWN)
    own[...] = total[:, :256].astype(jnp.bfloat16)
    other[...] = total[:, 256:].astype(jnp.bfloat16)


def flat_kernel(*refs):
    blocks, activations, (own, other) = refs[:12], refs[12:16], refs[16:]
    total = dot(rows_of(activations), rows_of(blocks), DOWN)
    own[...] = total[:128].astype(jnp.bfloat16)
    other[...] = total[128:].astype(jnp.bfloat16)


def weight_grads(kernel, blocks, hidden, kind, shape, block, index):
    parts = [b for four in blocks for b in four]
    width = hidden[0].shape[1]
    return pl.pallas_call(
        kernel,
        grid=(HALF // GRAD_TILE,),
        in_specs=[pl.BlockSpec((b.shape[0] // 2, GRAD_TILE), lambda i: (kind, i)) for b in parts]
        + [pl.BlockSpec((ROWS, width), lambda i: (0, 0)) for _ in hidden],
        out_specs=[pl.BlockSpec(block, index)] * 2,
        out_shape=[jax.ShapeDtypeStruct(shape, jnp.bfloat16)] * 2,
        compiler_params=params(40),
        cost_estimate=COST,
    )(*parts, *hidden)


def tall_grads(blocks, deltas):
    return weight_grads(tall_kernel, blocks, deltas, 0, (HALF, 256), (GRAD_TILE, 256), lambda i: (i, 0))


def flat_grads(blocks, activations):
    return weight_grads(flat_kernel, blocks, activations, 1, (128, HALF), (128, GRAD_TILE), lambda i: (0, i))


def on_device(tokens, out_grad, expert_ids, gates, w_gate, w_up, w_down):
    node = lax.axis_index("node")
    core = node % 2
    sizes = [hi - lo for lo, hi in PARTS]
    small, middle, large = ([o[i] for o in ORDERS] for i in range(3))

    experts = jnp.arange(WIDE - HALF, dtype=jnp.int32)[None, :]
    gate_sum = jnp.zeros((TOK, WIDE - HALF), jnp.float32)
    for k in range(4):
        gate_sum = gate_sum + jnp.where(expert_ids[:, k : k + 1] == experts, gates[:, k : k + 1].astype(jnp.float32), 0.0)
    gate_sum = jnp.concatenate([jnp.zeros_like(gate_sum), gate_sum], 0).astype(jnp.bfloat16)
    both = jnp.concatenate([tokens, out_grad], 0)
    other = swap(jnp.concatenate([half(both, 1 - core, 1), gate_sum], 1))
    rows = jnp.concatenate([jnp.concatenate([half(both, core, 1), gate_sum], 1), other], 0)
    units = move(place(core, pick_first), rows)
    units = [units[p * UNIT : (p + 1) * UNIT] for p in range(3)]

    def gathered(units, axes, beside):
        first = hops(units, axes, 0)
        if beside:
            first[0], beside = stage(first[0], beside)
        pairs = [jnp.concatenate([u, f], 0) for u, f in zip(units, first)]
        return pairs, hops(pairs, axes, 1), beside

    pairs, others, _ = gathered(units, small, ())
    units = [
        move(place(core, pick_joined(n, UNIT, 80)), jnp.concatenate([p, s], 0))
        for n, p, s in zip(sizes, pairs, others)
    ]
    units[2], raw = stage(units[2], (w_gate[0], w_up[0], w_down[0]))
    w_own = jnp.concatenate([half(raw[0], core, 0), half(raw[1], core, 0)], 1)
    w_other = jnp.concatenate([half(raw[0], 1 - core, 0), half(raw[1], 1 - core, 0)], 1)
    d_own, d_other = half(raw[2], core, 1), half(raw[2], 1 - core, 1)
    pairs, others, (w_own, w_other, d_own, d_other) = gathered(units, middle, [w_own, w_other, d_own, d_other])
    w_other, d_other = swap(w_other), swap(d_other)
    units = [
        move(place(core, pick_joined(4 * n, 80, 32 * n)), jnp.concatenate([p, s], 0))
        for n, p, s in zip(sizes, pairs, others)
    ]
    weights = (w_own, w_other, d_own, d_other)

    wanted = jnp.stack([node, node + 1 - 2 * core])
    chosen = jnp.arange(128)[None, :] == jnp.array([0, 1])[:, None]
    chosen = jnp.sum(
        (jnp.arange(128)[:, None, None] == wanted[None, :, None]) & chosen[None], axis=1
    ).astype(jnp.bfloat16)

    def paced(values, behind):
        pairs = [stage(v, b) for v, b in zip(values, behind)]
        return [p[0] for p in pairs], [p[1] for p in pairs]

    own, sums, done = units, [None] * 4, [None] * 4
    first = hops(own, large, 0)
    sums[0] = forward(own, weights)
    done[0] = backward(sums[0][0], swap(sums[0][1]), own, chosen, weights)
    own, done[0] = stage(own, done[0])
    own, first = paced(own, first)

    second, sums[1] = hops(own, large, 1), forward(first, weights)
    arrived = swap(sums[1][1])
    first, sums[1], arrived = stage(first, sums[1], arrived)
    first, second = paced(first, second)

    far, sums[2] = hops(first, large, 1), forward(second, weights)
    done[2] = backward(sums[2][0], arrived, second, chosen, weights)
    done[1] = backward(sums[1][0], swap(sums[2][1]), first, chosen, weights, 44)
    done[2], done[1] = stage(done[2], done[1])
    pieces, far = paced(done[2][2:], far)

    from_second, sums[3] = hops(pieces, large, 1), forward(far, weights, 44)
    done[3] = backward(sums[3][0], swap(sums[3][1]), far, chosen, weights, 44)
    from_second, done[3] = stage(from_second, done[3])

    every = [own, first, second, far]
    from_far, d_grad = stage(hops(done[3][2:], large, 1), flat_grads(every, [d[1] for d in done]))
    totals = [added(t, f) for t, f in zip(done[1][2:], from_far)]
    from_first, w_grad, d_arrived = stage(hops(totals, large, 0), tall_grads(every, [d[0] for d in done]), swap(d_grad[1]))
    totals = [added(t, s, f) for t, s, f in zip(done[0][2:], from_second, from_first)]

    def reduced(totals, axes, blocks, held, padded, beside):
        outer = [move(place(core, pick_split(n, h, padded, (2, 3))), t) for n, h, t in zip(blocks, held, totals)]
        far = hops(outer, axes, 1)
        inner = [move(place(core, pick_split(n, h, padded, (0, 1))), t) for n, h, t in zip(blocks, held, totals)]
        middle = [added(t[padded:], f[padded:]) for t, f in zip(inner, far)]
        first, beside = stage(hops(middle, axes, 0), beside)
        return [added(t[:padded], f[:padded], g) for t, f, g in zip(inner, far, first)], beside

    totals, w_arrived = reduced(
        totals, middle, [4 * n for n in sizes], [16 * n for n in sizes], 40, swap(w_grad[1])
    )
    w_grad = joined(w_grad[0], w_arrived, core, 0)
    down_grad = joined(d_grad[0], d_arrived, core, 1)
    totals, (w_grad, down_grad) = reduced(totals, small, sizes, [40] * 3, 16, (w_grad, down_grad))
    finished = move(place(core, pick_last), jnp.concatenate(totals, 0))
    arrived = swap(finished[16 : 16 + TOK])
    input_grad = joined(finished[:TOK], arrived, core, 1)
    return input_grad, w_grad[:, :128][None], w_grad[:, 128:][None], down_grad[None]


def solution(mesh):
    rows, deep, wide = P(ALL, None), P("node", None, "blk"), P("node", "blk", None)
    return jax.shard_map(
        on_device,
        mesh=mesh,
        in_specs=(rows, rows, rows, rows, deep, deep, wide),
        out_specs=(rows, deep, deep, wide),
        check_vma=False,
    )
```
